32 devices in a mesh: layer: 4 (over y, core), trace: 8 (over z, x).
Axes of the slice: x: 2, y: 2, z: 4, core: 2. Of those that a mesh axis runs over, the one named last changes fastest.
Arguments:
- source_up: bfloat16 [4, 8192, 256], P('layer', 'trace'), may hold values from -6 to 6
- source_down: bfloat16 [4, 8192, 256], P('layer', 'trace'), may hold values from -6 to 6
- diag_up: bfloat16 [4, 2, 8192, 1024], P('layer', None, 'trace'), may hold values from -0.125 to 0.125
- diag_down: bfloat16 [4, 2, 8192, 1024], P('layer', None, 'trace'), may hold values from -0.125 to 0.125
- projection: bfloat16 [4, 2, 32, 8192], P('layer', None, None, 'trace'), may hold values from -0.1875 to 0.1875
- expansion: bfloat16 [4, 2, 32, 8192], P('layer', None, None, 'trace'), may hold values from -1 to 1
- coupling: bfloat16 [4, 2, 2, 256, 256], P('layer', None, None, 'trace'), may hold values from -0.25 to 0.25
Outputs:
- trace_up: bfloat16 [4, 8192, 256], P('layer', 'trace')
- trace_down: bfloat16 [4, 8192, 256], P('layer', 'trace')
The draws below stay inside these ranges and needn't reach their ends.
All inputs are finite; a program needn't handle non-finite values.
Results may differ from the reference program's by a relative error of at most 0.013.
Values may be sent and summed in bfloat16 or wider, within the bound.
No kernel may reach another device: no remote copies, remote signals or barrier semaphores. Data moves between devices by JAX's collectives and lax.ppermute only.
A program may use at most 64 MiB of HBM per device.

```python
import jax
import jax.numpy as jnp
from jax import lax

P_DEV = 1024
K = 32
SRC = 128
ITERS = 3
GROUPS = 4
POINTS = 8192
KTOT = 256
N_TRACE = 8


def block_levels(own_key, extent, pieces, low, top_value):
    def one(position, shards_of):
        draws = jax.random.uniform(jax.random.fold_in(jax.random.fold_in(own_key, 6), position), (shards_of,), jnp.float32, low / len(pieces), top_value / len(pieces))
        return jnp.repeat(jnp.exp(draws), extent[position] // shards_of).reshape((-1,) + (1,) * (len(extent) - position - 1))

    gain = one(*pieces[0])
    for cut in pieces[1:]:
        gain = gain * one(*cut)
    return gain


def scatter_about(stream_key, shape, deviation, reach, pieces=(), dtype=jnp.bfloat16):
    level = block_levels(stream_key, shape, pieces, -0.22, 0.18) if pieces else 1.0
    values = jax.random.normal(stream_key, shape, jnp.float32) * deviation * level
    return jnp.minimum(jnp.maximum(values, -reach), reach).astype(dtype)


def setup_inputs(seed: int = 0) -> dict:
    streams_of = jax.random.split(jax.random.key(seed), 8)
    source_up = scatter_about(streams_of[0], (GROUPS, POINTS, 2 * SRC), 1.0, 6.0, ((0, 4), (1, 8)))
    source_down = scatter_about(streams_of[1], (GROUPS, POINTS, 2 * SRC), 1.0, 6.0, ((0, 4), (1, 8)))
    diag_up = scatter_about(streams_of[2], (GROUPS, 2, POINTS, P_DEV), (2 * P_DEV) ** -0.5, 0.125, ((0, 4), (2, 8)))
    diag_down = scatter_about(streams_of[3], (GROUPS, 2, POINTS, P_DEV), (2 * P_DEV) ** -0.5, 0.125, ((0, 4), (2, 8)))
    projection = scatter_about(streams_of[4], (GROUPS, 2, K, POINTS), P_DEV ** -0.5, 0.1875, ((0, 4), (3, 8)))
    expansion = scatter_about(streams_of[5], (GROUPS, 2, K, POINTS), K ** -0.5, 1.0, ((0, 4), (3, 8)))
    coupling = scatter_about(streams_of[6], (GROUPS, 2, 2, KTOT, KTOT), (2 * KTOT) ** -0.5, 0.25, ((0, 4), (3, 8)))
    return {"source_up": source_up, "source_down": source_down, "diag_up": diag_up, "diag_down": diag_down, "projection": projection, "expansion": expansion, "coupling": coupling}


def rotate(field):
    half = field.shape[-1] // 2
    return jnp.concatenate([-field[..., half:], field[..., :half]], axis=-1)


def layer_result(operands):
    field, block, basis_in, basis_out, couple = operands
    owners = N_TRACE
    values = field.astype(jnp.float32).reshape(owners, P_DEV, -1)
    proj = basis_in.astype(jnp.float32).reshape(K, owners, P_DEV)
    coeffs = jnp.einsum('kop,ops->oks', proj, values).reshape(owners * K, -1).astype(jnp.bfloat16)
    gathered = coeffs.astype(jnp.float32)
    coupled = jnp.dot(couple[0].astype(jnp.float32), gathered) + jnp.dot(couple[1].astype(jnp.float32), rotate(gathered))
    coupled = coupled.astype(jnp.bfloat16).astype(jnp.float32).reshape(owners, K, -1)
    expand = basis_out.astype(jnp.float32).reshape(K, owners, P_DEV)
    dense = block.astype(jnp.float32).reshape(2, owners, P_DEV, P_DEV)
    result = jnp.einsum('opq,oqs->ops', dense[0], values)
    result = result + jnp.einsum('opq,oqs->ops', dense[1], rotate(values))
    result = result + jnp.einsum('kop,oks->ops', expand, coupled)
    return result.reshape(owners * P_DEV, -1).astype(jnp.bfloat16)


def reference(source_up, source_down, diag_up, diag_down, projection, expansion, coupling):
    upward = source_up
    downward = source_down
    for step in range(ITERS):
        result_up = lax.map(layer_result, (upward, diag_up, projection[:, 0], expansion[:, 0], coupling[:, 0]))
        result_down = lax.map(layer_result, (downward, diag_down, projection[:, 1], expansion[:, 1], coupling[:, 1]))
        zeros = jnp.zeros_like(result_up[:1])
        arrived_up = jnp.concatenate([zeros, result_up[:-1]], axis=0)
        arrived_down = jnp.concatenate([result_down[1:], zeros], axis=0)
        upward = (source_up.astype(jnp.float32) + arrived_up.astype(jnp.float32)).astype(jnp.bfloat16)
        downward = (source_down.astype(jnp.float32) + arrived_down.astype(jnp.float32)).astype(jnp.bfloat16)
    return upward, downward
```

```python
import jax
import jax.numpy as jnp
from jax import lax
from jax.experimental import pallas as pl
from jax.experimental.pallas import tpu as pltpu
from jax.sharding import PartitionSpec as P

ITERS = 3
BF16 = jnp.bfloat16
F32 = jnp.float32


def rotate(field):
    half = field.shape[-1] // 2
    return jnp.concatenate([-field[..., half:], field[..., :half]], axis=-1)


def dot(a, b):
    return jnp.dot(a, b, preferred_element_type=F32)


def shifted(value, axis, steps):
    count = lax.axis_size(axis)
    initial, last = (max(0, -steps), min(count, count - steps))
    return lax.ppermute(value, axis, [(source, source + steps) for source in range(initial, last)])


def jacobi(source_up, source_down, diag_up, diag_down, projection, expansion, coupling):
    sources = (source_up[0], source_down[0])
    blocks = (diag_up[0], diag_down[0])
    fields = sources
    for step in range(ITERS):
        coeffs = [dot(projection[0, d], fields[d]).astype(BF16) for d in range(2)]
        gathered = lax.all_gather(jnp.stack(coeffs), "trace", axis=1, tiled=True)
        arrived = []
        for d in range(2):
            coupled = dot(coupling[0, d, 0], gathered[d])
            coupled = (coupled + dot(coupling[0, d, 1], rotate(gathered[d]))).astype(BF16)
            result = dot(blocks[d][0], fields[d]) + dot(blocks[d][1], rotate(fields[d]))
            result = result + lax.dot_general(
                expansion[0, d], coupled, (((0,), (0,)), ((), ())), preferred_element_type=F32
            )
            arrived.append(shifted(result.astype(BF16), "layer", 1 - 2 * d))
        fields = tuple(
            (sources[d].astype(F32) + arrived[d].astype(F32)).astype(BF16) for d in range(2)
        )
    return fields[0][None], fields[1][None]


CHUNKS = 4
HBM = pl.BlockSpec(memory_space=pltpu.HBM)
VMEM = pl.BlockSpec(memory_space=pltpu.VMEM)


def call(body, outs, far, near, scratch, sems, flops=0, moved=0):
    kept = [isinstance(out, tuple) for out in outs]
    return pl.pallas_call(
        body,
        out_shape=tuple(pltpu.VMEM(*out) if keep else out for out, keep in zip(outs, kept)),
        in_specs=[HBM] * len(far) + [VMEM] * len(near),
        out_specs=tuple(VMEM if keep else HBM for keep in kept),
        scratch_shapes=[pltpu.VMEM(shape, BF16) for shape in scratch]
        + [pltpu.SemaphoreType.DMA((sems,))],
        cost_estimate=pl.CostEstimate(flops=flops, bytes_accessed=moved, transcendentals=0),
        compiler_params=pltpu.CompilerParams(vmem_limit_bytes=24 * 2**20),
    )(*far, *near)


def roles():
    layer, layers = lax.axis_index("layer"), lax.axis_size("layer")
    outer = jnp.logical_or(layer == 0, layer == layers - 1)
    return outer, jnp.where(layer >= layers // 2, 1, 0)


def start(source, target, sem):
    copy = pltpu.make_async_copy(source, target, sem)
    copy.start()
    return copy


def pick(which, up_ref, down_ref, target, sem):
    @pl.when(which == 0)
    def _():
        start(up_ref, target, sem)

    @pl.when(which != 0)
    def _():
        start(down_ref, target, sem)


def arrive(target, sem):
    pltpu.make_async_copy(target, target, sem).wait()


def chunk(c, size):
    step = size // CHUNKS
    return pl.ds(pl.multiple_of(c * step, step), step)


def each_chunk(size, body):
    def one(c, carry):
        body(c, chunk(c, size))
        return carry

    lax.fori_loop(0, CHUNKS, one, 0)


def load_block(which, up_ref, down_ref, block, sems, base):
    def one(c, rows):
        pick(
            which,
            up_ref.at[0, :, rows, :],
            down_ref.at[0, :, rows, :],
            block.at[:, rows, :],
            sems.at[base + c],
        )

    each_chunk(block.shape[1], one)


def block_rows(block, rows, field, turned):
    return dot(block[0, rows, :], field[...]) + dot(block[1, rows, :], turned[...])


def dot_rows(a, b):
    return lax.dot_general(a, b, (((1,), (1,)), ((), ())), preferred_element_type=F32)


def expand(basis, coupled):
    return lax.dot_general(basis, coupled, (((0,), (0,)), ((), ())), preferred_element_type=F32)


def fold(wide, target, base):
    k, width = wide.shape[0], target.shape[1]
    for p in range(wide.shape[1] // width):
        target[base + p * k : base + (p + 1) * k, :] = wide[:, p * width : (p + 1) * width]


def unfold(source, base, k, points):
    width = source.shape[1]
    rows = [source[base + p * k : base + (p + 1) * k, :] for p in range(points // width)]
    return jnp.concatenate(rows, axis=1)


def first_kernel(
    sup, sdn, proj, expn, coup,
    payload, pack, source1, own, expn1, couple1,
    other, after, source2, coeffs, sems,
):
    outer, first = roles()
    second = 1 - first
    k, points, total = proj.shape[2], proj.shape[3], coup.shape[4]
    owners, width = payload.shape[0], source1.shape[1]
    start(coup.at[0, first], couple1, sems.at[0])
    start(proj.at[0, first], own, sems.at[1])
    pick(first, sup.at[0], sdn.at[0], source1, sems.at[2])
    start(expn.at[0, first], expn1, sems.at[3])

    @pl.when(outer)
    def _():
        arrive(own, sems.at[1])
        arrive(source1, sems.at[2])
        coeffs[...] = dot(own[...], source1[...]).astype(BF16)
        for o in range(owners):
            start(coeffs, payload.at[o, 0, :, pl.ds(0, width)], sems.at[4])
        arrive(couple1, sems.at[0])
        arrive(expn1, sems.at[3])
        arrive(payload.at[:, 0, :, pl.ds(0, width)], sems.at[4])

    @pl.when(jnp.logical_not(outer))
    def _():
        start(proj.at[0, second], other, sems.at[5])
        start(coup.at[0, second], after, sems.at[6])
        pick(second, sup.at[0], sdn.at[0], source2, sems.at[7])
        arrive(couple1, sems.at[0])
        for o in range(owners):
            start(couple1, payload.at[o, :, :, pl.ds(0, total)], sems.at[4])
        arrive(expn1, sems.at[3])
        arrive(other, sems.at[5])
        arrive(after, sems.at[6])
        pack[:k, :points] = other[...]
        for part in range(2):
            pack[k:, part * total : (part + 1) * total] = after[part]
        arrive(source2, sems.at[7])
        beyond = dot(other[...], source2[...]).astype(BF16)
        pack[k:, 2 * total : 2 * total + width] = beyond
        arrive(own, sems.at[1])
        arrive(source1, sems.at[2])
        arrive(payload.at[:, :, :, pl.ds(0, total)], sems.at[4])


def outer_apply_kernel(dup, ddn, source1, *refs):
    hops, (block, turned, sems) = refs[:CHUNKS], refs[CHUNKS:]
    outer, first = roles()

    @pl.when(outer)
    def _():
        load_block(first, dup, ddn, block, sems, 0)
        step = source1.shape[0] // CHUNKS
        turned[...] = rotate(source1[...])
        for c, hop in enumerate(hops):
            rows = pl.ds(c * step, step)
            arrive(block.at[:, rows, :], sems.at[c])
            hop[...] = block_rows(block, rows, source1, turned).astype(BF16)


def inner_prepare_kernel(dup, ddn, *refs):
    arrived, refs = refs[:CHUNKS], refs[CHUNKS:]
    packed, source1, own, expn1, before, sums, mixed, block, field, turned, sems = refs
    outer, first = roles()

    @pl.when(jnp.logical_not(outer))
    def _():
        load_block(first, dup, ddn, block, sems, 0)
        k, points = own.shape

        step = points // CHUNKS
        for c, part in enumerate(arrived):
            rows = slice(c * step, (c + 1) * step)
            value = (source1[rows, :].astype(F32) + part[...].astype(F32)).astype(BF16)
            field[rows, :] = value
            turned[rows, :] = rotate(value)
        other = packed[:k, :points]
        sums[:k, :] = dot(own[...], field[...])
        mixed[:, :k] = dot_rows(other, expn1[...]).astype(BF16)
        mixed[:, k : 2 * k] = dot_rows(own[...], before[...]).astype(BF16)
        parts = [0.0, 0.0]
        for c in range(CHUNKS):
            rows = pl.ds(c * step, step)
            arrive(block.at[:, rows, :], sems.at[c])
            for part in range(2):
                columns = other[:, c * step : (c + 1) * step]
                parts[part] = parts[part] + dot(columns, block[part, rows, :])
        parts = [part.astype(BF16) for part in parts]
        sums[k:, :] = dot(parts[0], field[...]) + dot(parts[1], turned[...])
        for part in range(2):
            place = (2 + part) * k
            mixed[:, place : place + k] = dot_rows(parts[part], before[...]).astype(BF16)


def outer_couple_kernel(gathered, couple1, mixed, out, sems):
    del mixed, sems
    outer, _ = roles()

    @pl.when(outer)
    def _():
        total = couple1.shape[2]
        coeffs = gathered[:, 0, :, : out.shape[1]].reshape(total, out.shape[1])
        out[...] = (dot(couple1[0], coeffs) + dot(couple1[1], rotate(coeffs))).astype(BF16)


def inner_gather_kernel(before, sums, mixed, packed, payload, small, sems):
    outer, _ = roles()

    @pl.when(jnp.logical_not(outer))
    def _():
        k, width = before.shape
        half, place = k // 2, 2 * k * payload.shape[0]
        coeffs = before[...]
        small[:k, :] = (sums[:k, :] + dot(mixed[:, k : 2 * k], coeffs)).astype(BF16)
        added = dot(mixed[:, 2 * k : 3 * k], coeffs)
        added = added + dot(mixed[:, 3 * k : 4 * k], rotate(coeffs))
        added = added + packed[k:, place : place + width].astype(F32)
        small[k : 2 * k, :] = (sums[k:, :] + added).astype(BF16)
        small[2 * k :, :k] = mixed[:half, :k]
        small[2 * k :, k : 2 * k] = mixed[half:, :k]
        for o in range(payload.shape[0]):
            start(small, payload.at[o], sems.at[0])
        arrive(payload, sems.at[0])


def inner_apply_kernel(dup, ddn, payload, *refs):
    del payload
    arrived, refs = refs[:CHUNKS], refs[CHUNKS:]
    before, other, expn1, source1, product, trace, block, turned, sems = refs
    outer, first = roles()

    @pl.when(jnp.logical_not(outer))
    def _():
        load_block(first, dup, ddn, block, sems, 0)
        points = source1.shape[0]
        step = points // CHUNKS
        fold(expn1[...], product, points)
        added = expand(other[...], before[...])
        for c, part in enumerate(arrived):
            rows = slice(c * step, (c + 1) * step)
            value = source1[rows, :].astype(F32) + part[...].astype(F32)
            value = (value + added[rows, :]).astype(BF16)
            trace[rows, :] = value
            turned[rows, :] = rotate(value)

        def one(c, rows):
            arrive(block.at[:, rows, :], sems.at[c])
            product[rows, :] = block_rows(block, rows, trace, turned).astype(BF16)

        each_chunk(points, one)


def inner_couple_kernel(gathered, second, packed, couple1, out, inner, later, sems):
    del sems
    outer, _ = roles()

    @pl.when(jnp.logical_not(outer))
    def _():
        owners, width = second.shape[0], second.shape[2]
        k, total = couple1.shape[1:]
        coeffs = second[:, :k, :].reshape(total, width)
        turned = rotate(coeffs)
        real = gathered[:, 0, :, :total].reshape(total, total)
        imag = gathered[:, 1, :, :total].reshape(total, total)
        inner[...] = (dot(real, coeffs) + dot(imag, turned)).astype(BF16)
        out[:k, :] = (dot(couple1[0], coeffs) + dot(couple1[1], turned)).astype(BF16)
        for o in range(owners):
            rows = slice(o * k, (o + 1) * k)
            own = inner[rows, :]
            added = [dot(second[o, 2 * k :, h * k : (h + 1) * k], own) for h in range(2)]
            added = jnp.concatenate(added, axis=0)
            later[rows, :] = (second[o, k : 2 * k, :].astype(F32) + added).astype(BF16)
        coeffs = later[...]
        result = dot(packed[k:, :total], coeffs)
        result = result + dot(packed[k:, total : 2 * total], rotate(coeffs))
        out[k:, :] = result.astype(BF16)


def settle_kernel(sup, sdn, expn, dup, ddn, coupled, block2, expn2, source2, sems):
    del coupled
    outer, first = roles()
    pick(1 - first, sup.at[0], sdn.at[0], source2, sems.at[CHUNKS + 1])

    @pl.when(jnp.logical_not(outer))
    def _():
        start(expn.at[0, 1 - first], expn2, sems.at[CHUNKS])
        load_block(1 - first, dup, ddn, block2, sems, 0)
        arrive(expn2, sems.at[CHUNKS])
        each_chunk(
            block2.shape[1], lambda c, rows: arrive(block2.at[:, rows, :], sems.at[c])
        )

    arrive(source2, sems.at[CHUNKS + 1])


def inner_second_kernel(
    crossed, coupled, source2, block2, expn2, out, trace, turned, sems
):
    del sems
    outer, _ = roles()

    @pl.when(jnp.logical_not(outer))
    def _():
        k, points = expn2.shape
        step = points // CHUNKS
        added = expand(unfold(crossed, points, k, points), coupled[:k, :])
        for c in range(CHUNKS):
            rows = slice(c * step, (c + 1) * step)
            value = source2[rows, :].astype(F32) + crossed[rows, :].astype(F32)
            value = (value + added[rows, :]).astype(BF16)
            trace[rows, :] = value
            turned[rows, :] = rotate(value)
        out[...] = expand(expn2[...], coupled[k:, :]).astype(BF16)

        def apply(c, rows):
            value = block_rows(block2, rows, trace, turned) + out[rows, :].astype(F32)
            out[rows, :] = value.astype(BF16)

        each_chunk(points, apply)


def last_kernel(arrived, one, two, source1, source2, up, down, sums, sems):
    outer, first = roles()

    def put(which, source, sem):
        @pl.when(which == 0)
        def _():
            start(source, up.at[0], sem)

        @pl.when(which != 0)
        def _():
            start(source, down.at[0], sem)

    @pl.when(outer)
    def _():
        put(first, source1, sems.at[0])

        def add(c, rows):
            value = source2[rows, :].astype(F32) + arrived[rows, :].astype(F32)
            sums[rows, :] = value.astype(BF16)

        each_chunk(sums.shape[0], add)
        put(1 - first, sums, sems.at[1])

    @pl.when(jnp.logical_not(outer))
    def _():
        put(first, one, sems.at[0])
        put(1 - first, two, sems.at[1])

    arrive(sums, sems.at[0])
    arrive(sums, sems.at[1])


def wave(*arrays):
    layers, owners = lax.axis_size("layer"), lax.axis_size("trace")
    source_up, source_down, diag_up, diag_down, projection, expansion, coupling = (
        pltpu.with_memory_space_constraint(array, pltpu.HBM) for array in arrays
    )
    _, points, width = source_up.shape
    k, total = projection.shape[2], coupling.shape[4]
    swap = [(g, g ^ 1) for g in range(layers)]
    across = [(g, layers - 1 - g) for g in range(layers)]
    inside = across[1:-1]
    folded = k * points // width

    def like(*shape):
        return jax.ShapeDtypeStruct(shape, BF16)

    def kept(*shape, of=BF16):
        return shape, of

    field, block, basis, couple = (points, width), (2, points, points), (k, points), (2, k, total)
    small = dict(flops=2 * k * points * width, moved=4 * points * width)
    large = dict(flops=4 * points * points * width, moved=4 * points * points)
    diagonals = (diag_up, diag_down)
    packing = max(points, 2 * total + width)

    payload, pack, source1, own, expn1, couple1 = call(
        first_kernel,
        (
            like(owners, 2, k, max(total, width)),
            *(kept(2 * k, packing), kept(*field), kept(*basis), kept(*basis), kept(*couple)),
        ),
        (source_up, source_down, projection, expansion, coupling),
        (),
        [basis, couple, field, (k, width)],
        8,
        **small,
    )
    gathered = lax.all_to_all(payload, "trace", 0, 0)
    packed = lax.ppermute(pack, "layer", across)
    other = lax.ppermute(expn1, "layer", swap)
    hops = call(
        outer_apply_kernel,
        (kept(points // CHUNKS, width),) * CHUNKS,
        diagonals,
        (source1,),
        [block, field],
        CHUNKS,
        **large,
    )
    arrived = [lax.ppermute(hop, "layer", swap) for hop in hops]
    sums, mixed = call(
        inner_prepare_kernel,
        (kept(2 * k, width, of=F32), kept(k, 4 * k)),
        diagonals,
        (*arrived, packed, source1, own, expn1, other),
        [block, field, field],
        CHUNKS,
        **large,
    )
    (before,) = call(
        outer_couple_kernel, (kept(k, width),), (), (gathered, couple1, mixed), [], 1, **small
    )
    before = lax.ppermute(before, "layer", swap)
    (payload,) = call(
        inner_gather_kernel,
        (like(owners, 2 * k + k // 2, width),),
        (),
        (before, sums, mixed, packed),
        [(2 * k + k // 2, width)],
        1,
        **small,
    )
    second = lax.all_to_all(payload, "trace", 0, 0)
    product, one = call(
        inner_apply_kernel,
        (kept(points + folded, width), kept(*field)),
        (*diagonals, payload),
        (*arrived, before, other, expn1, source1),
        [block, field],
        CHUNKS,
        **large,
    )
    crossed = lax.ppermute(product, "layer", inside)
    (coupled,) = call(
        inner_couple_kernel,
        (kept(2 * k, width),),
        (),
        (gathered, second, packed, couple1),
        [(total, width), (total, width)],
        1,
        **small,
    )
    reached = lax.ppermute(coupled, "layer", across)
    block2, expn2, source2 = call(
        settle_kernel,
        (kept(*block), kept(*basis), kept(*field)),
        (source_up, source_down, expansion, *diagonals),
        (coupled,),
        [],
        CHUNKS + 2,
        **large,
    )
    result, two = call(
        inner_second_kernel,
        (kept(*field), kept(*field)),
        (),
        (crossed, reached, source2, block2, expn2),
        [field],
        1,
        **large,
    )
    arrived = lax.ppermute(result, "layer", swap)
    return call(
        last_kernel,
        (like(1, *field), like(1, *field)),
        (),
        (arrived, one, two, source1, source2),
        [field],
        2,
        **small,
    )


def solution(mesh):
    shards = wave if mesh.shape["layer"] == ITERS + 1 else jacobi
    return jax.shard_map(
        shards,
        mesh=mesh,
        in_specs=(
            P("layer", "trace", None),
            P("layer", "trace", None),
            P("layer", None, "trace", None),
            P("layer", None, "trace", None),
            P("layer", None, None, "trace"),
            P("layer", None, None, "trace"),
            P("layer", None, None, "trace", None),
        ),
        out_specs=(P("layer", "trace", None), P("layer", "trace", None)),
        check_vma=False,
    )
```

```python
import jax
import jax.numpy as jnp
from jax import lax
from jax.experimental import pallas as pl
from jax.experimental.pallas import tpu as pltpu
from jax.sharding import PartitionSpec as P

ITERS = 3
BF16 = jnp.bfloat16
F32 = jnp.float32


def rotate(field):
    half = field.shape[-1] // 2
    return jnp.concatenate([-field[..., half:], field[..., :half]], axis=-1)


def dot(a, b):
    return jnp.dot(a, b, preferred_element_type=F32)


def shifted(value, axis, steps):
    count = lax.axis_size(axis)
    initial, last = (max(0, -steps), min(count, count - steps))
    return lax.ppermute(value, axis, [(source, source + steps) for source in range(initial, last)])


def jacobi(source_up, source_down, diag_up, diag_down, projection, expansion, coupling):
    sources = (source_up[0], source_down[0])
    blocks = (diag_up[0], diag_down[0])
    fields = sources
    for step in range(ITERS):
        coeffs = [dot(projection[0, d], fields[d]).astype(BF16) for d in range(2)]
        gathered = lax.all_gather(jnp.stack(coeffs), "trace", axis=1, tiled=True)
        arrived = []
        for d in range(2):
            coupled = dot(coupling[0, d, 0], gathered[d])
            coupled = (coupled + dot(coupling[0, d, 1], rotate(gathered[d]))).astype(BF16)
            result = dot(blocks[d][0], fields[d]) + dot(blocks[d][1], rotate(fields[d]))
            result = result + lax.dot_general(
                expansion[0, d], coupled, (((0,), (0,)), ((), ())), preferred_element_type=F32
            )
            arrived.append(shifted(result.astype(BF16), "layer", 1 - 2 * d))
        fields = tuple(
            (sources[d].astype(F32) + arrived[d].astype(F32)).astype(BF16) for d in range(2)
        )
    return fields[0][None], fields[1][None]


CHUNKS = 4
HBM = pl.BlockSpec(memory_space=pltpu.HBM)
VMEM = pl.BlockSpec(memory_space=pltpu.VMEM)


def call(body, outs, far, near, scratch, sems, flops=0, moved=0):
    kept = [isinstance(out, tuple) for out in outs]
    return pl.pallas_call(
        body,
        out_shape=tuple(pltpu.VMEM(*out) if keep else out for out, keep in zip(outs, kept)),
        in_specs=[HBM] * len(far) + [VMEM] * len(near),
        out_specs=tuple(VMEM if keep else HBM for keep in kept),
        scratch_shapes=[pltpu.VMEM(shape, BF16) for shape in scratch]
        + [pltpu.SemaphoreType.DMA((sems,))],
        cost_estimate=pl.CostEstimate(flops=flops, bytes_accessed=moved, transcendentals=0),
        compiler_params=pltpu.CompilerParams(vmem_limit_bytes=24 * 2**20),
    )(*far, *near)


def roles():
    layer, layers = lax.axis_index("layer"), lax.axis_size("layer")
    outer = jnp.logical_or(layer == 0, layer == layers - 1)
    return outer, jnp.where(layer >= layers // 2, 1, 0)


def start(source, target, sem):
    copy = pltpu.make_async_copy(source, target, sem)
    copy.start()
    return copy


def pick(which, up_ref, down_ref, target, sem):
    @pl.when(which == 0)
    def _():
        start(up_ref, target, sem)

    @pl.when(which != 0)
    def _():
        start(down_ref, target, sem)


def arrive(target, sem):
    pltpu.make_async_copy(target, target, sem).wait()


def chunk(c, size):
    step = size // CHUNKS
    return pl.ds(pl.multiple_of(c * step, step), step)


def each_chunk(size, body):
    def one(c, carry):
        body(c, chunk(c, size))
        return carry

    lax.fori_loop(0, CHUNKS, one, 0)


def load_block(which, up_ref, down_ref, block, sems, base):
    def one(c, rows):
        pick(
            which,
            up_ref.at[0, :, rows, :],
            down_ref.at[0, :, rows, :],
            block.at[:, rows, :],
            sems.at[base + c],
        )

    each_chunk(block.shape[1], one)


def block_rows(block, rows, field, turned):
    return dot(block[0, rows, :], field[...]) + dot(block[1, rows, :], turned[...])


def dot_rows(a, b):
    return lax.dot_general(a, b, (((1,), (1,)), ((), ())), preferred_element_type=F32)


def expand(basis, coupled):
    return lax.dot_general(basis, coupled, (((0,), (0,)), ((), ())), preferred_element_type=F32)


def first_kernel(
    sup, sdn, proj, expn, coup,
    payload, pack, source1, own, expn1, couple1,
    other, after, source2, coeffs, sems,
):
    outer, first = roles()
    second = 1 - first
    k, points, total = proj.shape[2], proj.shape[3], coup.shape[4]
    owners, width = payload.shape[0], source1.shape[1]
    start(coup.at[0, first], couple1, sems.at[0])
    start(proj.at[0, first], own, sems.at[1])
    pick(first, sup.at[0], sdn.at[0], source1, sems.at[2])
    start(expn.at[0, first], expn1, sems.at[3])

    @pl.when(outer)
    def _():
        arrive(own, sems.at[1])
        arrive(source1, sems.at[2])
        coeffs[...] = dot(own[...], source1[...]).astype(BF16)
        for o in range(owners):
            start(coeffs, payload.at[o, 0, :, pl.ds(0, width)], sems.at[4])
        arrive(couple1, sems.at[0])
        arrive(expn1, sems.at[3])
        arrive(payload.at[:, 0, :, pl.ds(0, width)], sems.at[4])

    @pl.when(jnp.logical_not(outer))
    def _():
        start(proj.at[0, second], other, sems.at[5])
        start(coup.at[0, second], after, sems.at[6])
        pick(second, sup.at[0], sdn.at[0], source2, sems.at[7])
        arrive(couple1, sems.at[0])
        for o in range(owners):
            start(couple1, payload.at[o, :, :, pl.ds(0, total)], sems.at[4])
        arrive(expn1, sems.at[3])
        arrive(other, sems.at[5])
        arrive(after, sems.at[6])
        pack[:k, :points] = other[...]
        pack[2 * k :, :points] = expn1[...]
        for part in range(2):
            pack[k : 2 * k, part * total : (part + 1) * total] = after[part]
        arrive(source2, sems.at[7])
        beyond = dot(other[...], source2[...]).astype(BF16)
        pack[k : 2 * k, 2 * total : 2 * total + width] = beyond
        arrive(own, sems.at[1])
        arrive(source1, sems.at[2])
        arrive(payload.at[:, :, :, pl.ds(0, total)], sems.at[4])


def outer_apply_kernel(dup, ddn, source1, *refs):
    hops, (block, turned, result, sems) = refs[:CHUNKS], refs[CHUNKS:]
    outer, first = roles()

    @pl.when(outer)
    def _():
        load_block(first, dup, ddn, block, sems, 0)
        step = source1.shape[0] // CHUNKS
        turned[...] = rotate(source1[...])

        def one(c, rows):
            arrive(block.at[:, rows, :], sems.at[c])
            result[rows, :] = block_rows(block, rows, source1, turned).astype(BF16)

        each_chunk(source1.shape[0], one)
        for c, hop in enumerate(hops):
            hop[...] = result[c * step : (c + 1) * step, :]


def inner_prepare_kernel(dup, ddn, *refs):
    arrived, refs = refs[:CHUNKS], refs[CHUNKS:]
    packed, source1, own, expn1, before, sums, mixed, block, field, turned, sems = refs
    outer, first = roles()

    @pl.when(jnp.logical_not(outer))
    def _():
        load_block(first, dup, ddn, block, sems, 0)
        k, points = own.shape

        step = points // CHUNKS
        for c, part in enumerate(arrived):
            rows = slice(c * step, (c + 1) * step)
            value = (source1[rows, :].astype(F32) + part[...].astype(F32)).astype(BF16)
            field[rows, :] = value
            turned[rows, :] = rotate(value)
        other = packed[:k, :points]
        sums[:k, :] = dot(own[...], field[...])
        mixed[:, :k] = dot_rows(other, expn1[...]).astype(BF16)
        mixed[:, k : 2 * k] = dot_rows(own[...], before[...]).astype(BF16)
        parts = [0.0, 0.0]
        for c in range(CHUNKS):
            rows = pl.ds(c * step, step)
            arrive(block.at[:, rows, :], sems.at[c])
            for part in range(2):
                columns = other[:, c * step : (c + 1) * step]
                parts[part] = parts[part] + dot(columns, block[part, rows, :])
        parts = [part.astype(BF16) for part in parts]
        sums[k:, :] = dot(parts[0], field[...]) + dot(parts[1], turned[...])
        for part in range(2):
            place = (2 + part) * k
            mixed[:, place : place + k] = dot_rows(parts[part], before[...]).astype(BF16)


def outer_couple_kernel(gathered, couple1, out, sems):
    del sems
    outer, _ = roles()

    @pl.when(outer)
    def _():
        total = couple1.shape[2]
        coeffs = gathered[:, 0, :, : out.shape[1]].reshape(total, out.shape[1])
        out[...] = (dot(couple1[0], coeffs) + dot(couple1[1], rotate(coeffs))).astype(BF16)


def inner_gather_kernel(before, sums, mixed, packed, payload, small, sems):
    outer, _ = roles()

    @pl.when(jnp.logical_not(outer))
    def _():
        k, width = before.shape
        half, place = k // 2, 2 * k * payload.shape[0]
        coeffs = before[...]
        small[:k, :] = (sums[:k, :] + dot(mixed[:, k : 2 * k], coeffs)).astype(BF16)
        added = dot(mixed[:, 2 * k : 3 * k], coeffs)
        added = added + dot(mixed[:, 3 * k : 4 * k], rotate(coeffs))
        added = added + packed[k : 2 * k, place : place + width].astype(F32)
        small[k : 2 * k, :] = (sums[k:, :] + added).astype(BF16)
        small[2 * k :, :k] = mixed[:half, :k]
        small[2 * k :, k : 2 * k] = mixed[half:, :k]
        for o in range(payload.shape[0]):
            start(small, payload.at[o], sems.at[0])
        arrive(payload, sems.at[0])


def inner_apply_kernel(dup, ddn, payload, *refs):
    del payload
    arrived, refs = refs[:CHUNKS], refs[CHUNKS:]
    before, other, source1, product, trace, block, turned, sems = refs
    outer, first = roles()

    @pl.when(jnp.logical_not(outer))
    def _():
        load_block(first, dup, ddn, block, sems, 0)
        points = source1.shape[0]
        step = points // CHUNKS
        added = expand(other[...], before[...])
        for c, part in enumerate(arrived):
            rows = slice(c * step, (c + 1) * step)
            value = source1[rows, :].astype(F32) + part[...].astype(F32)
            value = (value + added[rows, :]).astype(BF16)
            trace[rows, :] = value
            turned[rows, :] = rotate(value)

        def one(c, rows):
            arrive(block.at[:, rows, :], sems.at[c])
            product[rows, :] = block_rows(block, rows, trace, turned).astype(BF16)

        each_chunk(points, one)


def inner_couple_kernel(gathered, second, packed, couple1, out, inner, later, sems):
    del sems
    outer, _ = roles()

    @pl.when(jnp.logical_not(outer))
    def _():
        owners, width = second.shape[0], second.shape[2]
        k, total = couple1.shape[1:]
        coeffs = second[:, :k, :].reshape(total, width)
        turned = rotate(coeffs)
        real = gathered[:, 0, :, :total].reshape(total, total)
        imag = gathered[:, 1, :, :total].reshape(total, total)
        inner[...] = (dot(real, coeffs) + dot(imag, turned)).astype(BF16)
        out[:k, :] = (dot(couple1[0], coeffs) + dot(couple1[1], turned)).astype(BF16)
        for o in range(owners):
            rows = slice(o * k, (o + 1) * k)
            own = inner[rows, :]
            added = [dot(second[o, 2 * k :, h * k : (h + 1) * k], own) for h in range(2)]
            added = jnp.concatenate(added, axis=0)
            later[rows, :] = (second[o, k : 2 * k, :].astype(F32) + added).astype(BF16)
        coeffs = later[...]
        result = dot(packed[k : 2 * k, :total], coeffs)
        result = result + dot(packed[k : 2 * k, total : 2 * total], rotate(coeffs))
        out[k:, :] = result.astype(BF16)


def load_part(first_chunk, which, up_ref, down_ref, block, size, sems, base):
    for c in range(block.shape[1] // size):
        source = pl.ds((first_chunk + c) * size, size)
        pick(
            which,
            up_ref.at[0, :, source, :],
            down_ref.at[0, :, source, :],
            block.at[:, pl.ds(c * size, size), :],
            sems.at[base + c],
        )


def each_chunk_of(block, size, body):
    def one(c, carry):
        body(c, pl.ds(pl.multiple_of(c * size, size), size))
        return carry

    lax.fori_loop(0, block.shape[1] // size, one, 0)


def settle_kernel(
    sup, sdn, expn, dup, ddn, coupled, packed, lower, bases, source2, sems
):
    del coupled
    outer, first = roles()
    pick(1 - first, sup.at[0], sdn.at[0], source2, sems.at[0])

    @pl.when(jnp.logical_not(outer))
    def _():
        k, points = bases.shape[0] // 2, bases.shape[1]
        start(expn.at[0, 1 - first], bases.at[pl.ds(k, k), :], sems.at[1])
        step = points // CHUNKS
        load_part(0, 1 - first, dup, ddn, lower, step, sems, 2)
        bases[:k, :] = packed[2 * k :, :points]
        arrive(bases.at[pl.ds(k, k), :], sems.at[1])
        each_chunk_of(
            lower, step, lambda c, rows: arrive(lower.at[:, rows, :], sems.at[2 + c])
        )

    arrive(source2, sems.at[0])


def inner_second_kernel(
    dup, ddn, crossed, coupled, source2, lower, bases,
    out, trace, turned, upper, sems,
):
    outer, first = roles()

    @pl.when(jnp.logical_not(outer))
    def _():
        k, points = coupled.shape[0] // 2, bases.shape[1]
        step = points // CHUNKS
        load_part(CHUNKS // 2, 1 - first, dup, ddn, upper, step, sems, 0)

        added = expand(bases[:k, :], coupled[:k, :])
        for c in range(CHUNKS):
            rows = slice(c * step, (c + 1) * step)
            value = source2[rows, :].astype(F32) + crossed[rows, :].astype(F32)
            value = (value + added[rows, :]).astype(BF16)
            trace[rows, :] = value
            turned[rows, :] = rotate(value)
        out[...] = expand(bases[k:, :], coupled[k:, :]).astype(BF16)

        def put(block, rows, base):
            place = pl.ds(pl.multiple_of(rows.start + base, step), step)
            value = block_rows(block, rows, trace, turned) + out[place, :].astype(F32)
            out[place, :] = value.astype(BF16)

        each_chunk_of(lower, step, lambda c, rows: put(lower, rows, 0))

        def second(c, rows):
            arrive(upper.at[:, rows, :], sems.at[c])
            put(upper, rows, points // 2)

        each_chunk_of(upper, step, second)


def last_kernel(arrived, one, two, source1, source2, up, down, sums, sems):
    outer, first = roles()

    def put(which, source, sem):
        @pl.when(which == 0)
        def _():
            start(source, up.at[0], sem)

        @pl.when(which != 0)
        def _():
            start(source, down.at[0], sem)

    def put_rows(which, rows, sem):
        @pl.when(which == 0)
        def _():
            start(sums.at[rows, :], up.at[0, rows, :], sem)

        @pl.when(which != 0)
        def _():
            start(sums.at[rows, :], down.at[0, rows, :], sem)

    @pl.when(outer)
    def _():
        put(first, source1, sems.at[0])

        def add(c, rows):
            value = source2[rows, :].astype(F32) + arrived[rows, :].astype(F32)
            sums[rows, :] = value.astype(BF16)
            put_rows(1 - first, rows, sems.at[1])

        each_chunk(sums.shape[0], add)

    @pl.when(jnp.logical_not(outer))
    def _():
        put(first, one, sems.at[0])
        put(1 - first, two, sems.at[1])

    arrive(sums, sems.at[0])
    arrive(sums, sems.at[1])


def wave(*arrays):
    layers, owners = lax.axis_size("layer"), lax.axis_size("trace")
    source_up, source_down, diag_up, diag_down, projection, expansion, coupling = (
        pltpu.with_memory_space_constraint(array, pltpu.HBM) for array in arrays
    )
    _, points, width = source_up.shape
    k, total = projection.shape[2], coupling.shape[4]
    swap = [(g, g ^ 1) for g in range(layers)]
    across = [(g, layers - 1 - g) for g in range(layers)]
    inside = across[1:-1]

    def like(*shape):
        return jax.ShapeDtypeStruct(shape, BF16)

    def kept(*shape, of=BF16):
        return shape, of

    field, block, basis, couple = (points, width), (2, points, points), (k, points), (2, k, total)
    small = dict(flops=2 * k * points * width, moved=4 * points * width)
    large = dict(flops=4 * points * points * width, moved=4 * points * points)
    diagonals = (diag_up, diag_down)
    packing = max(points, 2 * total + width)

    payload, pack, source1, own, expn1, couple1 = call(
        first_kernel,
        (
            like(owners, 2, k, max(total, width)),
            *(kept(3 * k, packing), kept(*field), kept(*basis), kept(*basis), kept(*couple)),
        ),
        (source_up, source_down, projection, expansion, coupling),
        (),
        [basis, couple, field, (k, width)],
        8,
        **small,
    )
    gathered = lax.all_to_all(payload, "trace", 0, 0)
    packed = lax.ppermute(pack, "layer", across)
    other = lax.ppermute(expn1, "layer", swap)
    hops = call(
        outer_apply_kernel,
        (kept(points // CHUNKS, width),) * CHUNKS,
        diagonals,
        (source1,),
        [block, field, field],
        CHUNKS,
        **large,
    )
    arrived = [lax.ppermute(hop, "layer", swap) for hop in hops]
    sums, mixed = call(
        inner_prepare_kernel,
        (kept(2 * k, width, of=F32), kept(k, 4 * k)),
        diagonals,
        (*arrived, packed, source1, own, expn1, other),
        [block, field, field],
        CHUNKS,
        **large,
    )
    (before,) = call(
        outer_couple_kernel, (kept(k, width),), (), (gathered, couple1), [], 1, **small
    )
    before = lax.ppermute(before, "layer", swap)
    (payload,) = call(
        inner_gather_kernel,
        (like(owners, 2 * k + k // 2, width),),
        (),
        (before, sums, mixed, packed),
        [(2 * k + k // 2, width)],
        1,
        **small,
    )
    second = lax.all_to_all(payload, "trace", 0, 0)
    product, one = call(
        inner_apply_kernel,
        (kept(*field), kept(*field)),
        (*diagonals, payload),
        (*arrived, before, other, source1),
        [block, field],
        CHUNKS,
        **large,
    )
    crossed = lax.ppermute(product, "layer", across)
    (coupled,) = call(
        inner_couple_kernel,
        (kept(2 * k, width),),
        (),
        (gathered, second, packed, couple1),
        [(total, width), (total, width)],
        1,
        **small,
    )
    reached = lax.ppermute(coupled, "layer", across)
    lower, bases, source2 = call(
        settle_kernel,
        (kept(2, points // 2, points), kept(2 * k, points), kept(*field)),
        (source_up, source_down, expansion, *diagonals),
        (coupled, packed),
        [],
        2 + CHUNKS // 2,
        **large,
    )
    result, two = call(
        inner_second_kernel,
        (kept(*field), kept(*field)),
        diagonals,
        (crossed, reached, source2, lower, bases),
        [field, (2, points // 2, points)],
        CHUNKS // 2,
        **large,
    )
    arrived = lax.ppermute(result, "layer", swap)
    return call(
        last_kernel,
        (like(1, *field), like(1, *field)),
        (),
        (arrived, one, two, source1, source2),
        [field],
        2,
        **small,
    )


def solution(mesh):
    shards = wave if mesh.shape["layer"] == ITERS + 1 else jacobi
    return jax.shard_map(
        shards,
        mesh=mesh,
        in_specs=(
            P("layer", "trace", None),
            P("layer", "trace", None),
            P("layer", None, "trace", None),
            P("layer", None, "trace", None),
            P("layer", None, None, "trace"),
            P("layer", None, None, "trace"),
            P("layer", None, None, "trace", None),
        ),
        out_specs=(P("layer", "trace", None), P("layer", "trace", None)),
        check_vma=False,
    )
```

```python
import jax
import jax.numpy as jnp
from jax import lax
from jax.experimental import pallas as pl
from jax.experimental.pallas import tpu as pltpu
from jax.sharding import PartitionSpec as P

ITERS = 3
BF16 = jnp.bfloat16
F32 = jnp.float32


def rotate(field):
    half = field.shape[-1] // 2
    return jnp.concatenate([-field[..., half:], field[..., :half]], axis=-1)


def dot(a, b):
    return jnp.dot(a, b, preferred_element_type=F32)


def shifted(value, axis, steps):
    count = lax.axis_size(axis)
    initial, last = (max(0, -steps), min(count, count - steps))
    return lax.ppermute(value, axis, [(source, source + steps) for source in range(initial, last)])


def jacobi(source_up, source_down, diag_up, diag_down, projection, expansion, coupling):
    sources = (source_up[0], source_down[0])
    blocks = (diag_up[0], diag_down[0])
    fields = sources
    for step in range(ITERS):
        coeffs = [dot(projection[0, d], fields[d]).astype(BF16) for d in range(2)]
        gathered = lax.all_gather(jnp.stack(coeffs), "trace", axis=1, tiled=True)
        arrived = []
        for d in range(2):
            coupled = dot(coupling[0, d, 0], gathered[d])
            coupled = (coupled + dot(coupling[0, d, 1], rotate(gathered[d]))).astype(BF16)
            result = dot(blocks[d][0], fields[d]) + dot(blocks[d][1], rotate(fields[d]))
            result = result + lax.dot_general(
                expansion[0, d], coupled, (((0,), (0,)), ((), ())), preferred_element_type=F32
            )
            arrived.append(shifted(result.astype(BF16), "layer", 1 - 2 * d))
        fields = tuple(
            (sources[d].astype(F32) + arrived[d].astype(F32)).astype(BF16) for d in range(2)
        )
    return fields[0][None], fields[1][None]


CHUNKS = 4
HBM = pl.BlockSpec(memory_space=pltpu.HBM)
VMEM = pl.BlockSpec(memory_space=pltpu.VMEM)


def call(body, outs, far, near, scratch, sems, flops=0, moved=0):
    kept = [isinstance(out, tuple) for out in outs]
    return pl.pallas_call(
        body,
        out_shape=tuple(pltpu.VMEM(*out) if keep else out for out, keep in zip(outs, kept)),
        in_specs=[HBM] * len(far) + [VMEM] * len(near),
        out_specs=tuple(VMEM if keep else HBM for keep in kept),
        scratch_shapes=[pltpu.VMEM(shape, BF16) for shape in scratch]
        + [pltpu.SemaphoreType.DMA((sems,))],
        cost_estimate=pl.CostEstimate(flops=flops, bytes_accessed=moved, transcendentals=0),
        compiler_params=pltpu.CompilerParams(vmem_limit_bytes=24 * 2**20),
    )(*far, *near)


def roles():
    layer, layers = lax.axis_index("layer"), lax.axis_size("layer")
    outer = jnp.logical_or(layer == 0, layer == layers - 1)
    return outer, jnp.where(layer >= layers // 2, 1, 0)


def start(source, target, sem):
    copy = pltpu.make_async_copy(source, target, sem)
    copy.start()
    return copy


def pick(which, up_ref, down_ref, target, sem):
    @pl.when(which == 0)
    def _():
        start(up_ref, target, sem)

    @pl.when(which != 0)
    def _():
        start(down_ref, target, sem)


def arrive(target, sem):
    pltpu.make_async_copy(target, target, sem).wait()


def chunk(c, size):
    step = size // CHUNKS
    return pl.ds(pl.multiple_of(c * step, step), step)


def each_chunk(size, body):
    def one(c, carry):
        body(c, chunk(c, size))
        return carry

    lax.fori_loop(0, CHUNKS, one, 0)


def load_block(which, up_ref, down_ref, block, sems, base):
    def one(c, rows):
        pick(
            which,
            up_ref.at[0, :, rows, :],
            down_ref.at[0, :, rows, :],
            block.at[:, rows, :],
            sems.at[base + c],
        )

    each_chunk(block.shape[1], one)


def block_rows(block, rows, field, turned):
    return dot(block[0, rows, :], field[...]) + dot(block[1, rows, :], turned[...])


def dot_rows(a, b):
    return lax.dot_general(a, b, (((1,), (1,)), ((), ())), preferred_element_type=F32)


def expand(basis, coupled):
    return lax.dot_general(basis, coupled, (((0,), (0,)), ((), ())), preferred_element_type=F32)


def first_kernel(
    sup, sdn, proj, expn, coup,
    payload, pack, source1, own, expn1, couple1,
    other, after, source2, coeffs, sems,
):
    outer, first = roles()
    second = 1 - first
    k, points, total = proj.shape[2], proj.shape[3], coup.shape[4]
    owners, width = payload.shape[0], source1.shape[1]
    start(coup.at[0, first], couple1, sems.at[0])
    start(proj.at[0, first], own, sems.at[1])
    pick(first, sup.at[0], sdn.at[0], source1, sems.at[2])
    start(expn.at[0, first], expn1, sems.at[3])

    @pl.when(outer)
    def _():
        arrive(own, sems.at[1])
        arrive(source1, sems.at[2])
        coeffs[...] = dot(own[...], source1[...]).astype(BF16)
        for o in range(owners):
            start(coeffs, payload.at[o, 0, :, pl.ds(0, width)], sems.at[4])
        arrive(couple1, sems.at[0])
        arrive(expn1, sems.at[3])
        arrive(payload.at[:, 0, :, pl.ds(0, width)], sems.at[4])

    @pl.when(jnp.logical_not(outer))
    def _():
        start(proj.at[0, second], other, sems.at[5])
        start(coup.at[0, second], after, sems.at[6])
        pick(second, sup.at[0], sdn.at[0], source2, sems.at[7])
        arrive(couple1, sems.at[0])
        for o in range(owners):
            start(couple1, payload.at[o, :, :, pl.ds(0, total)], sems.at[4])
        arrive(expn1, sems.at[3])
        arrive(other, sems.at[5])
        arrive(after, sems.at[6])
        pack[:k, :points] = other[...]
        pack[2 * k :, :points] = expn1[...]
        for part in range(2):
            pack[k : 2 * k, part * total : (part + 1) * total] = after[part]
        arrive(source2, sems.at[7])
        beyond = dot(other[...], source2[...]).astype(BF16)
        pack[k : 2 * k, 2 * total : 2 * total + width] = beyond
        arrive(own, sems.at[1])
        arrive(source1, sems.at[2])
        arrive(payload.at[:, :, :, pl.ds(0, total)], sems.at[4])


def outer_apply_kernel(dup, ddn, source1, *refs):
    hops, (block, turned, result, sems) = refs[:CHUNKS], refs[CHUNKS:]
    outer, first = roles()
    load_block(first, dup, ddn, block, sems, 0)

    @pl.when(outer)
    def _():
        step = source1.shape[0] // CHUNKS
        turned[...] = rotate(source1[...])

        def one(c, rows):
            arrive(block.at[:, rows, :], sems.at[c])
            result[rows, :] = block_rows(block, rows, source1, turned).astype(BF16)

        each_chunk(source1.shape[0], one)
        for c, hop in enumerate(hops):
            hop[...] = result[c * step : (c + 1) * step, :]

    @pl.when(jnp.logical_not(outer))
    def _():
        each_chunk(
            block.shape[1], lambda c, rows: arrive(block.at[:, rows, :], sems.at[c])
        )


def inner_mix_kernel(block, packed, own, expn1, before, basis, mixed, sems):
    del sems
    outer, _ = roles()

    @pl.when(jnp.logical_not(outer))
    def _():
        k, points = own.shape
        other = packed[:k, :points]
        mixed[:, :k] = dot_rows(other, expn1[...]).astype(BF16)
        step = points // CHUNKS
        parts = [0.0, 0.0]
        for c in range(CHUNKS):
            rows = pl.ds(c * step, step)
            for part in range(2):
                columns = other[:, c * step : (c + 1) * step]
                parts[part] = parts[part] + dot(columns, block[part, rows, :])
        basis[:k, :] = own[...]
        for part in range(2):
            basis[(1 + part) * k : (2 + part) * k, :] = parts[part].astype(BF16)
        value = dot_rows(basis[...], before[...]).astype(BF16)
        for part in range(3):
            mixed[:, (1 + part) * k : (2 + part) * k] = value[part * k : (part + 1) * k, :]


def inner_prepare_kernel(*refs):
    arrived, refs = refs[:CHUNKS], refs[CHUNKS:]
    source1, basis, sums, field, turned, sems = refs
    del sems
    outer, _ = roles()

    @pl.when(jnp.logical_not(outer))
    def _():
        k, points = basis.shape[0] // 3, basis.shape[1]
        step = points // CHUNKS
        for c, part in enumerate(arrived):
            rows = slice(c * step, (c + 1) * step)
            value = (source1[rows, :].astype(F32) + part[...].astype(F32)).astype(BF16)
            field[rows, :] = value
            turned[rows, :] = rotate(value)
        sums[...] = dot(basis[: 2 * k, :], field[...])
        sums[k:, :] += dot(basis[2 * k :, :], turned[...])


def outer_couple_kernel(gathered, couple1, mixed, out, sems):
    del mixed, sems
    outer, _ = roles()

    @pl.when(outer)
    def _():
        total = couple1.shape[2]
        coeffs = gathered[:, 0, :, : out.shape[1]].reshape(total, out.shape[1])
        out[...] = (dot(couple1[0], coeffs) + dot(couple1[1], rotate(coeffs))).astype(BF16)


def inner_gather_kernel(before, sums, mixed, packed, payload, small, sems):
    outer, _ = roles()

    @pl.when(jnp.logical_not(outer))
    def _():
        k, width = before.shape
        half, place = k // 2, 2 * k * payload.shape[0]
        coeffs = before[...]
        small[:k, :] = (sums[:k, :] + dot(mixed[:, k : 2 * k], coeffs)).astype(BF16)
        added = dot(mixed[:, 2 * k : 3 * k], coeffs)
        added = added + dot(mixed[:, 3 * k : 4 * k], rotate(coeffs))
        added = added + packed[k : 2 * k, place : place + width].astype(F32)
        small[k : 2 * k, :] = (sums[k:, :] + added).astype(BF16)
        small[2 * k :, :k] = mixed[:half, :k]
        small[2 * k :, k : 2 * k] = mixed[half:, :k]
        for o in range(payload.shape[0]):
            start(small, payload.at[o], sems.at[0])
        arrive(payload, sems.at[0])


def inner_apply_kernel(dup, ddn, payload, *refs):
    del payload
    arrived, refs = refs[:CHUNKS], refs[CHUNKS:]
    before, other, source1, product, trace, block, turned, sems = refs
    outer, first = roles()

    @pl.when(jnp.logical_not(outer))
    def _():
        load_block(first, dup, ddn, block, sems, 0)
        points = source1.shape[0]
        step = points // CHUNKS
        added = expand(other[...], before[...])
        for c, part in enumerate(arrived):
            rows = slice(c * step, (c + 1) * step)
            value = source1[rows, :].astype(F32) + part[...].astype(F32)
            value = (value + added[rows, :]).astype(BF16)
            trace[rows, :] = value
            turned[rows, :] = rotate(value)

        def one(c, rows):
            arrive(block.at[:, rows, :], sems.at[c])
            product[rows, :] = block_rows(block, rows, trace, turned).astype(BF16)

        each_chunk(points, one)


def inner_couple_kernel(gathered, second, packed, couple1, out, inner, later, sems):
    del sems
    outer, _ = roles()

    @pl.when(jnp.logical_not(outer))
    def _():
        owners, width = second.shape[0], second.shape[2]
        k, total = couple1.shape[1:]
        coeffs = second[:, :k, :].reshape(total, width)
        turned = rotate(coeffs)
        real = gathered[:, 0, :, :total].reshape(total, total)
        imag = gathered[:, 1, :, :total].reshape(total, total)
        inner[...] = (dot(real, coeffs) + dot(imag, turned)).astype(BF16)
        out[:k, :] = (dot(couple1[0], coeffs) + dot(couple1[1], turned)).astype(BF16)
        for o in range(owners):
            rows = slice(o * k, (o + 1) * k)
            own = inner[rows, :]
            added = [dot(second[o, 2 * k :, h * k : (h + 1) * k], own) for h in range(2)]
            added = jnp.concatenate(added, axis=0)
            later[rows, :] = (second[o, k : 2 * k, :].astype(F32) + added).astype(BF16)
        coeffs = later[...]
        result = dot(packed[k : 2 * k, :total], coeffs)
        result = result + dot(packed[k : 2 * k, total : 2 * total], rotate(coeffs))
        out[k:, :] = result.astype(BF16)


def load_part(first_chunk, which, up_ref, down_ref, block, size, sems, base):
    for c in range(block.shape[1] // size):
        source = pl.ds((first_chunk + c) * size, size)
        pick(
            which,
            up_ref.at[0, :, source, :],
            down_ref.at[0, :, source, :],
            block.at[:, pl.ds(c * size, size), :],
            sems.at[base + c],
        )


def each_chunk_of(block, size, body):
    def one(c, carry):
        body(c, pl.ds(pl.multiple_of(c * size, size), size))
        return carry

    lax.fori_loop(0, block.shape[1] // size, one, 0)


def settle_kernel(
    sup, sdn, expn, dup, ddn, coupled, packed, lower, bases, source2, sems
):
    del coupled
    outer, first = roles()
    pick(1 - first, sup.at[0], sdn.at[0], source2, sems.at[0])

    @pl.when(jnp.logical_not(outer))
    def _():
        k, points = bases.shape[0] // 2, bases.shape[1]
        start(expn.at[0, 1 - first], bases.at[pl.ds(k, k), :], sems.at[1])
        step = points // CHUNKS
        load_part(0, 1 - first, dup, ddn, lower, step, sems, 2)
        bases[:k, :] = packed[2 * k :, :points]
        arrive(bases.at[pl.ds(k, k), :], sems.at[1])
        each_chunk_of(
            lower, step, lambda c, rows: arrive(lower.at[:, rows, :], sems.at[2 + c])
        )

    arrive(source2, sems.at[0])


def inner_second_kernel(
    dup, ddn, crossed, coupled, source2, lower, bases,
    out, trace, turned, upper, sems,
):
    outer, first = roles()

    @pl.when(jnp.logical_not(outer))
    def _():
        k, points = coupled.shape[0] // 2, bases.shape[1]
        step = points // CHUNKS
        load_part(CHUNKS // 2, 1 - first, dup, ddn, upper, step, sems, 0)

        added = expand(bases[:k, :], coupled[:k, :])
        for c in range(CHUNKS):
            rows = slice(c * step, (c + 1) * step)
            value = source2[rows, :].astype(F32) + crossed[rows, :].astype(F32)
            value = (value + added[rows, :]).astype(BF16)
            trace[rows, :] = value
            turned[rows, :] = rotate(value)
        out[...] = expand(bases[k:, :], coupled[k:, :]).astype(BF16)

        def put(block, rows, base):
            place = pl.ds(pl.multiple_of(rows.start + base, step), step)
            value = block_rows(block, rows, trace, turned) + out[place, :].astype(F32)
            out[place, :] = value.astype(BF16)

        each_chunk_of(lower, step, lambda c, rows: put(lower, rows, 0))

        def second(c, rows):
            arrive(upper.at[:, rows, :], sems.at[c])
            put(upper, rows, points // 2)

        each_chunk_of(upper, step, second)


def last_kernel(arrived, one, two, source1, source2, up, down, sums, sems):
    outer, first = roles()

    def put(which, source, sem):
        @pl.when(which == 0)
        def _():
            start(source, up.at[0], sem)

        @pl.when(which != 0)
        def _():
            start(source, down.at[0], sem)

    def put_rows(which, rows, sem):
        @pl.when(which == 0)
        def _():
            start(sums.at[rows, :], up.at[0, rows, :], sem)

        @pl.when(which != 0)
        def _():
            start(sums.at[rows, :], down.at[0, rows, :], sem)

    @pl.when(outer)
    def _():
        put(first, source1, sems.at[0])

        def add(c, rows):
            value = source2[rows, :].astype(F32) + arrived[rows, :].astype(F32)
            sums[rows, :] = value.astype(BF16)
            put_rows(1 - first, rows, sems.at[1])

        each_chunk(sums.shape[0], add)

    @pl.when(jnp.logical_not(outer))
    def _():
        put(first, one, sems.at[0])
        put(1 - first, two, sems.at[1])

    arrive(sums, sems.at[0])
    arrive(sums, sems.at[1])


def wave(*arrays):
    layers, owners = lax.axis_size("layer"), lax.axis_size("trace")
    source_up, source_down, diag_up, diag_down, projection, expansion, coupling = (
        pltpu.with_memory_space_constraint(array, pltpu.HBM) for array in arrays
    )
    _, points, width = source_up.shape
    k, total = projection.shape[2], coupling.shape[4]
    swap = [(g, g ^ 1) for g in range(layers)]
    across = [(g, layers - 1 - g) for g in range(layers)]
    inside = across[1:-1]

    def like(*shape):
        return jax.ShapeDtypeStruct(shape, BF16)

    def kept(*shape, of=BF16):
        return shape, of

    field, block, basis, couple = (points, width), (2, points, points), (k, points), (2, k, total)
    small = dict(flops=2 * k * points * width, moved=4 * points * width)
    large = dict(flops=4 * points * points * width, moved=4 * points * points)
    diagonals = (diag_up, diag_down)
    packing = max(points, 2 * total + width)

    payload, pack, source1, own, expn1, couple1 = call(
        first_kernel,
        (
            like(owners, 2, k, max(total, width)),
            *(kept(3 * k, packing), kept(*field), kept(*basis), kept(*basis), kept(*couple)),
        ),
        (source_up, source_down, projection, expansion, coupling),
        (),
        [basis, couple, field, (k, width)],
        8,
        **small,
    )
    gathered = lax.all_to_all(payload, "trace", 0, 0)
    pairs = [(a * owners + o, b * owners + o) for a, b in inside for o in range(owners)]
    pairs += [(g * owners + o, g * owners + (o ^ 1)) for g in (0, layers - 1) for o in range(owners)]
    packed = lax.ppermute(pack, ("layer", "trace"), pairs)
    other = lax.ppermute(expn1, "layer", swap)
    *hops, block1 = call(
        outer_apply_kernel,
        (kept(points // CHUNKS, width),) * CHUNKS + (kept(*block),),
        diagonals,
        (source1,),
        [field, field],
        CHUNKS,
        **large,
    )
    arrived = [lax.ppermute(hop, "layer", swap) for hop in hops]
    basis1, mixed = call(
        inner_mix_kernel,
        (kept(3 * k, points), kept(k, 4 * k)),
        (),
        (block1, packed, own, expn1, other),
        [],
        1,
        **large,
    )
    (before,) = call(
        outer_couple_kernel, (kept(k, width),), (), (gathered, couple1, mixed), [], 1, **small
    )
    before = lax.ppermute(before, "layer", swap)
    (sums,) = call(
        inner_prepare_kernel,
        (kept(2 * k, width, of=F32),),
        (),
        (*arrived, source1, basis1),
        [field, field],
        1,
        **small,
    )
    (payload,) = call(
        inner_gather_kernel,
        (like(owners, 2 * k + k // 2, width),),
        (),
        (before, sums, mixed, packed),
        [(2 * k + k // 2, width)],
        1,
        **small,
    )
    half = owners // 2
    ends = [[g * owners + p * half + o for g in (0, layers - 1) for o in range(half)] for p in range(2)]
    groups = [[g * owners + o for o in range(owners)] for g in range(1, layers - 1)] + ends
    second = lax.all_to_all(payload, ("layer", "trace"), 0, 0, axis_index_groups=groups)
    product, one = call(
        inner_apply_kernel,
        (kept(*field), kept(*field)),
        (*diagonals, payload),
        (*arrived, before, other, source1),
        [block, field],
        CHUNKS,
        **large,
    )
    crossed = lax.ppermute(product, ("layer", "trace"), pairs)
    (coupled,) = call(
        inner_couple_kernel,
        (kept(2 * k, width),),
        (),
        (gathered, second, packed, couple1),
        [(total, width), (total, width)],
        1,
        **small,
    )
    reached = lax.ppermute(coupled, "layer", across)
    lower, bases, source2 = call(
        settle_kernel,
        (kept(2, points // 2, points), kept(2 * k, points), kept(*field)),
        (source_up, source_down, expansion, *diagonals),
        (coupled, packed),
        [],
        2 + CHUNKS // 2,
        **large,
    )
    result, two = call(
        inner_second_kernel,
        (kept(*field), kept(*field)),
        diagonals,
        (crossed, reached, source2, lower, bases),
        [field, (2, points // 2, points)],
        CHUNKS // 2,
        **large,
    )
    arrived = lax.ppermute(result, "layer", swap)
    return call(
        last_kernel,
        (like(1, *field), like(1, *field)),
        (),
        (arrived, one, two, source1, source2),
        [field],
        2,
        **small,
    )


def solution(mesh):
    shards = wave if mesh.shape["layer"] == ITERS + 1 else jacobi
    return jax.shard_map(
        shards,
        mesh=mesh,
        in_specs=(
            P("layer", "trace", None),
            P("layer", "trace", None),
            P("layer", None, "trace", None),
            P("layer", None, "trace", None),
            P("layer", None, None, "trace"),
            P("layer", None, None, "trace"),
            P("layer", None, None, "trace", None),
        ),
        out_specs=(P("layer", "trace", None), P("layer", "trace", None)),
        check_vma=False,
    )
```

```python
import jax
import jax.numpy as jnp
from jax import lax
from jax.experimental import pallas as pl
from jax.experimental.pallas import tpu as pltpu
from jax.sharding import PartitionSpec as P

ITERS = 3
BF16 = jnp.bfloat16
F32 = jnp.float32


def rotate(field):
    half = field.shape[-1] // 2
    return jnp.concatenate([-field[..., half:], field[..., :half]], axis=-1)


def dot(a, b):
    return jnp.dot(a, b, preferred_element_type=F32)


def shifted(value, axis, steps):
    count = lax.axis_size(axis)
    initial, last = (max(0, -steps), min(count, count - steps))
    return lax.ppermute(value, axis, [(source, source + steps) for source in range(initial, last)])


def jacobi(source_up, source_down, diag_up, diag_down, projection, expansion, coupling):
    sources = (source_up[0], source_down[0])
    blocks = (diag_up[0], diag_down[0])
    fields = sources
    for step in range(ITERS):
        coeffs = [dot(projection[0, d], fields[d]).astype(BF16) for d in range(2)]
        gathered = lax.all_gather(jnp.stack(coeffs), "trace", axis=1, tiled=True)
        arrived = []
        for d in range(2):
            coupled = dot(coupling[0, d, 0], gathered[d])
            coupled = (coupled + dot(coupling[0, d, 1], rotate(gathered[d]))).astype(BF16)
            result = dot(blocks[d][0], fields[d]) + dot(blocks[d][1], rotate(fields[d]))
            result = result + lax.dot_general(
                expansion[0, d], coupled, (((0,), (0,)), ((), ())), preferred_element_type=F32
            )
            arrived.append(shifted(result.astype(BF16), "layer", 1 - 2 * d))
        fields = tuple(
            (sources[d].astype(F32) + arrived[d].astype(F32)).astype(BF16) for d in range(2)
        )
    return fields[0][None], fields[1][None]


CHUNKS = 4
HBM = pl.BlockSpec(memory_space=pltpu.HBM)
VMEM = pl.BlockSpec(memory_space=pltpu.VMEM)


def call(body, outs, far, near, scratch, sems, flops=0, moved=0):
    kept = [isinstance(out, tuple) for out in outs]
    return pl.pallas_call(
        body,
        out_shape=tuple(pltpu.VMEM(*out) if keep else out for out, keep in zip(outs, kept)),
        in_specs=[HBM] * len(far) + [VMEM] * len(near),
        out_specs=tuple(VMEM if keep else HBM for keep in kept),
        scratch_shapes=[pltpu.VMEM(shape, BF16) for shape in scratch]
        + [pltpu.SemaphoreType.DMA((sems,))],
        cost_estimate=pl.CostEstimate(flops=flops, bytes_accessed=moved, transcendentals=0),
        compiler_params=pltpu.CompilerParams(vmem_limit_bytes=24 * 2**20),
    )(*far, *near)


def roles():
    layer, layers = lax.axis_index("layer"), lax.axis_size("layer")
    outer = jnp.logical_or(layer == 0, layer == layers - 1)
    return outer, jnp.where(layer >= layers // 2, 1, 0)


def start(source, target, sem):
    copy = pltpu.make_async_copy(source, target, sem)
    copy.start()
    return copy


def pick(which, up_ref, down_ref, target, sem):
    @pl.when(which == 0)
    def _():
        start(up_ref, target, sem)

    @pl.when(which != 0)
    def _():
        start(down_ref, target, sem)


def arrive(target, sem):
    pltpu.make_async_copy(target, target, sem).wait()


def chunk(c, size):
    step = size // CHUNKS
    return pl.ds(pl.multiple_of(c * step, step), step)


def each_chunk(size, body):
    def one(c, carry):
        body(c, chunk(c, size))
        return carry

    lax.fori_loop(0, CHUNKS, one, 0)


def load_block(which, up_ref, down_ref, block, sems, base):
    def one(c, rows):
        pick(
            which,
            up_ref.at[0, :, rows, :],
            down_ref.at[0, :, rows, :],
            block.at[:, rows, :],
            sems.at[base + c],
        )

    each_chunk(block.shape[1], one)


def block_rows(block, rows, field, turned):
    return dot(block[0, rows, :], field[...]) + dot(block[1, rows, :], turned[...])


def dot_rows(a, b):
    return lax.dot_general(a, b, (((1,), (1,)), ((), ())), preferred_element_type=F32)


def expand(basis, coupled):
    return lax.dot_general(basis, coupled, (((0,), (0,)), ((), ())), preferred_element_type=F32)


def first_kernel(
    sup, sdn, proj, expn, coup,
    payload, pack, source1, own, expn1, couple1,
    other, after, source2, coeffs, sems,
):
    outer, first = roles()
    second = 1 - first
    k, points, total = proj.shape[2], proj.shape[3], coup.shape[4]
    owners, width = payload.shape[0], source1.shape[1]
    start(coup.at[0, first], couple1, sems.at[0])
    start(proj.at[0, first], own, sems.at[1])
    pick(first, sup.at[0], sdn.at[0], source1, sems.at[2])
    start(expn.at[0, first], expn1, sems.at[3])

    @pl.when(outer)
    def _():
        arrive(own, sems.at[1])
        arrive(source1, sems.at[2])
        coeffs[...] = dot(own[...], source1[...]).astype(BF16)
        for o in range(owners):
            start(coeffs, payload.at[o, 0, :, pl.ds(0, width)], sems.at[4])
        arrive(couple1, sems.at[0])
        arrive(expn1, sems.at[3])
        arrive(payload.at[:, 0, :, pl.ds(0, width)], sems.at[4])

    @pl.when(jnp.logical_not(outer))
    def _():
        start(proj.at[0, second], other, sems.at[5])
        start(coup.at[0, second], after, sems.at[6])
        pick(second, sup.at[0], sdn.at[0], source2, sems.at[7])
        arrive(couple1, sems.at[0])
        for o in range(owners):
            start(couple1, payload.at[o, :, :, pl.ds(0, total)], sems.at[4])
        arrive(expn1, sems.at[3])
        arrive(other, sems.at[5])
        arrive(after, sems.at[6])
        pack[:k, :points] = other[...]
        pack[2 * k :, :points] = expn1[...]
        for part in range(2):
            pack[k : 2 * k, part * total : (part + 1) * total] = after[part]
        arrive(source2, sems.at[7])
        beyond = dot(other[...], source2[...]).astype(BF16)
        pack[k : 2 * k, 2 * total : 2 * total + width] = beyond
        arrive(own, sems.at[1])
        arrive(source1, sems.at[2])
        arrive(payload.at[:, :, :, pl.ds(0, total)], sems.at[4])


def outer_apply_kernel(dup, ddn, source1, *refs):
    hops, (block, turned, result, sems) = refs[:CHUNKS], refs[CHUNKS:]
    outer, first = roles()
    load_block(first, dup, ddn, block, sems, 0)

    @pl.when(outer)
    def _():
        step = source1.shape[0] // CHUNKS
        turned[...] = rotate(source1[...])

        def one(c, rows):
            arrive(block.at[:, rows, :], sems.at[c])
            result[rows, :] = block_rows(block, rows, source1, turned).astype(BF16)

        each_chunk(source1.shape[0], one)
        for c, hop in enumerate(hops):
            hop[...] = result[c * step : (c + 1) * step, :]

    @pl.when(jnp.logical_not(outer))
    def _():
        each_chunk(
            block.shape[1], lambda c, rows: arrive(block.at[:, rows, :], sems.at[c])
        )


def inner_mix_kernel(block, packed, own, expn1, before, basis, mixed, sems):
    del sems
    outer, _ = roles()

    @pl.when(jnp.logical_not(outer))
    def _():
        k, points = own.shape
        other = packed[:k, :points]
        mixed[:, :k] = dot_rows(other, expn1[...]).astype(BF16)
        step = points // CHUNKS
        parts = [0.0, 0.0]
        for c in range(CHUNKS):
            rows = pl.ds(c * step, step)
            for part in range(2):
                columns = other[:, c * step : (c + 1) * step]
                parts[part] = parts[part] + dot(columns, block[part, rows, :])
        basis[:k, :] = own[...]
        for part in range(2):
            basis[(1 + part) * k : (2 + part) * k, :] = parts[part].astype(BF16)
        value = dot_rows(basis[...], before[...]).astype(BF16)
        for part in range(3):
            mixed[:, (1 + part) * k : (2 + part) * k] = value[part * k : (part + 1) * k, :]


def inner_prepare_kernel(*refs):
    arrived, refs = refs[:CHUNKS], refs[CHUNKS:]
    source1, basis, sums, field, turned, sems = refs
    del sems
    outer, _ = roles()

    @pl.when(jnp.logical_not(outer))
    def _():
        k, points = basis.shape[0] // 3, basis.shape[1]
        step = points // CHUNKS
        for c, part in enumerate(arrived):
            rows = slice(c * step, (c + 1) * step)
            value = (source1[rows, :].astype(F32) + part[...].astype(F32)).astype(BF16)
            field[rows, :] = value
            turned[rows, :] = rotate(value)
        sums[...] = dot(basis[: 2 * k, :], field[...])
        sums[k:, :] += dot(basis[2 * k :, :], turned[...])


def outer_couple_kernel(gathered, couple1, mixed, out, sems):
    del mixed, sems
    outer, _ = roles()

    @pl.when(outer)
    def _():
        total = couple1.shape[2]
        coeffs = gathered[:, 0, :, : out.shape[1]].reshape(total, out.shape[1])
        out[...] = (dot(couple1[0], coeffs) + dot(couple1[1], rotate(coeffs))).astype(BF16)


def inner_gather_kernel(before, sums, mixed, packed, payload, small, sems):
    outer, _ = roles()

    @pl.when(jnp.logical_not(outer))
    def _():
        k, width = before.shape
        half, place = k // 2, 2 * k * payload.shape[0]
        coeffs = before[...]
        small[:k, :] = (sums[:k, :] + dot(mixed[:, k : 2 * k], coeffs)).astype(BF16)
        added = dot(mixed[:, 2 * k : 3 * k], coeffs)
        added = added + dot(mixed[:, 3 * k : 4 * k], rotate(coeffs))
        added = added + packed[k : 2 * k, place : place + width].astype(F32)
        small[k : 2 * k, :] = (sums[k:, :] + added).astype(BF16)
        small[2 * k :, :k] = mixed[:half, :k]
        small[2 * k :, k : 2 * k] = mixed[half:, :k]
        for o in range(payload.shape[0]):
            start(small, payload.at[o], sems.at[0])
        arrive(payload, sems.at[0])


def inner_apply_kernel(sup, sdn, dup, ddn, payload, *refs):
    del payload
    arrived, refs = refs[:CHUNKS], refs[CHUNKS:]
    before, other, source1, product, trace, source2, block, turned, sems = refs
    outer, first = roles()
    pick(1 - first, sup.at[0], sdn.at[0], source2, sems.at[CHUNKS])

    @pl.when(jnp.logical_not(outer))
    def _():
        load_block(first, dup, ddn, block, sems, 0)
        points = source1.shape[0]
        step = points // CHUNKS
        added = expand(other[...], before[...])
        for c, part in enumerate(arrived):
            rows = slice(c * step, (c + 1) * step)
            value = source1[rows, :].astype(F32) + part[...].astype(F32)
            value = (value + added[rows, :]).astype(BF16)
            trace[rows, :] = value
            turned[rows, :] = rotate(value)

        def one(c, rows):
            arrive(block.at[:, rows, :], sems.at[c])
            product[rows, :] = block_rows(block, rows, trace, turned).astype(BF16)

        each_chunk(points, one)

    arrive(source2, sems.at[CHUNKS])


def inner_couple_kernel(gathered, second, packed, couple1, out, inner, later, sems):
    del sems
    outer, _ = roles()

    @pl.when(jnp.logical_not(outer))
    def _():
        owners, width = second.shape[0], second.shape[2]
        k, total = couple1.shape[1:]
        coeffs = second[:, :k, :].reshape(total, width)
        turned = rotate(coeffs)
        real = gathered[:, 0, :, :total].reshape(total, total)
        imag = gathered[:, 1, :, :total].reshape(total, total)
        inner[...] = (dot(real, coeffs) + dot(imag, turned)).astype(BF16)
        out[:k, :] = (dot(couple1[0], coeffs) + dot(couple1[1], turned)).astype(BF16)
        for o in range(owners):
            rows = slice(o * k, (o + 1) * k)
            own = inner[rows, :]
            added = [dot(second[o, 2 * k :, h * k : (h + 1) * k], own) for h in range(2)]
            added = jnp.concatenate(added, axis=0)
            later[rows, :] = (second[o, k : 2 * k, :].astype(F32) + added).astype(BF16)
        coeffs = later[...]
        result = dot(packed[k : 2 * k, :total], coeffs)
        result = result + dot(packed[k : 2 * k, total : 2 * total], rotate(coeffs))
        out[k:, :] = result.astype(BF16)


def load_part(first_chunk, which, up_ref, down_ref, block, size, sems, base):
    for c in range(block.shape[1] // size):
        source = pl.ds((first_chunk + c) * size, size)
        pick(
            which,
            up_ref.at[0, :, source, :],
            down_ref.at[0, :, source, :],
            block.at[:, pl.ds(c * size, size), :],
            sems.at[base + c],
        )


def each_chunk_of(block, size, body):
    def one(c, carry):
        body(c, pl.ds(pl.multiple_of(c * size, size), size))
        return carry

    lax.fori_loop(0, block.shape[1] // size, one, 0)


def settle_kernel(
    expn, dup, ddn, coupled, packed, lower, bases, sems
):
    del coupled
    outer, first = roles()

    @pl.when(jnp.logical_not(outer))
    def _():
        k, points = bases.shape[0] // 2, bases.shape[1]
        start(expn.at[0, 1 - first], bases.at[pl.ds(k, k), :], sems.at[1])
        step = points // CHUNKS
        load_part(0, 1 - first, dup, ddn, lower, step, sems, 2)
        bases[:k, :] = packed[2 * k :, :points]
        arrive(bases.at[pl.ds(k, k), :], sems.at[1])
        each_chunk_of(
            lower, step, lambda c, rows: arrive(lower.at[:, rows, :], sems.at[2 + c])
        )


def inner_second_kernel(
    dup, ddn, crossed, coupled, source2, lower, bases,
    out, trace, turned, rest, tail, added2, upper, sems,
):
    outer, first = roles()

    @pl.when(jnp.logical_not(outer))
    def _():
        k, points = coupled.shape[0] // 2, bases.shape[1]
        step = points // CHUNKS
        load_part(CHUNKS // 2, 1 - first, dup, ddn, upper, step, sems, 0)
        load_part(CHUNKS - 1, 1 - first, dup, ddn, rest, step, sems, CHUNKS)

        added = expand(bases[:k, :], coupled[:k, :])
        for c in range(CHUNKS):
            rows = slice(c * step, (c + 1) * step)
            value = source2[rows, :].astype(F32) + crossed[rows, :].astype(F32)
            value = (value + added[rows, :]).astype(BF16)
            trace[rows, :] = value
            turned[rows, :] = rotate(value)
        added2[...] = expand(bases[k:, :], coupled[k:, :]).astype(BF16)
        tail[...] = added2[points - step :, :]

        def put(block, rows, base):
            place = pl.ds(pl.multiple_of(rows.start + base, step), step)
            value = block_rows(block, rows, trace, turned) + added2[place, :].astype(F32)
            out[place, :] = value.astype(BF16)

        each_chunk_of(lower, step, lambda c, rows: put(lower, rows, 0))

        def second(c, rows):
            arrive(upper.at[:, rows, :], sems.at[c])
            put(upper, rows, points // 2)

        each_chunk_of(upper, step, second)
        arrive(rest, sems.at[CHUNKS])


def inner_rest_kernel(rest, trace, turned, tail, out, sems):
    del sems
    outer, _ = roles()

    @pl.when(jnp.logical_not(outer))
    def _():
        value = dot(rest[0], trace[...]) + dot(rest[1], turned[...])
        out[...] = (value + tail[...].astype(F32)).astype(BF16)


def last_kernel(most, last, one, two, source1, source2, up, down, sums, sems):
    outer, first = roles()

    def put(which, source, sem):
        @pl.when(which == 0)
        def _():
            start(source, up.at[0], sem)

        @pl.when(which != 0)
        def _():
            start(source, down.at[0], sem)

    def put_rows(which, rows, sem):
        @pl.when(which == 0)
        def _():
            start(sums.at[rows, :], up.at[0, rows, :], sem)

        @pl.when(which != 0)
        def _():
            start(sums.at[rows, :], down.at[0, rows, :], sem)

    @pl.when(outer)
    def _():
        put(first, source1, sems.at[0])

        cut = most.shape[0]
        for part, rows in ((most, pl.ds(0, cut)), (last, pl.ds(cut, sums.shape[0] - cut))):
            value = source2[rows, :].astype(F32) + part[...].astype(F32)
            sums[rows, :] = value.astype(BF16)
            put_rows(1 - first, rows, sems.at[1])

    @pl.when(jnp.logical_not(outer))
    def _():
        put(first, one, sems.at[0])
        put(1 - first, two, sems.at[1])

    arrive(sums, sems.at[0])
    arrive(sums, sems.at[1])


def wave(*arrays):
    layers, owners = lax.axis_size("layer"), lax.axis_size("trace")
    source_up, source_down, diag_up, diag_down, projection, expansion, coupling = (
        pltpu.with_memory_space_constraint(array, pltpu.HBM) for array in arrays
    )
    _, points, width = source_up.shape
    k, total = projection.shape[2], coupling.shape[4]
    swap = [(g, g ^ 1) for g in range(layers)]
    across = [(g, layers - 1 - g) for g in range(layers)]
    inside = across[1:-1]

    def like(*shape):
        return jax.ShapeDtypeStruct(shape, BF16)

    def kept(*shape, of=BF16):
        return shape, of

    field, block, basis, couple = (points, width), (2, points, points), (k, points), (2, k, total)
    small = dict(flops=2 * k * points * width, moved=4 * points * width)
    large = dict(flops=4 * points * points * width, moved=4 * points * points)
    diagonals = (diag_up, diag_down)
    packing = max(points, 2 * total + width)

    payload, pack, source1, own, expn1, couple1 = call(
        first_kernel,
        (
            like(owners, 2, k, max(total, width)),
            *(kept(3 * k, packing), kept(*field), kept(*basis), kept(*basis), kept(*couple)),
        ),
        (source_up, source_down, projection, expansion, coupling),
        (),
        [basis, couple, field, (k, width)],
        8,
        **small,
    )
    gathered = lax.all_to_all(payload, "trace", 0, 0)
    pairs = [(a * owners + o, b * owners + o) for a, b in inside for o in range(owners)]
    pairs += [(g * owners + o, g * owners + (o ^ 1)) for g in (0, layers - 1) for o in range(owners)]
    packed = lax.ppermute(pack, ("layer", "trace"), pairs)
    other = lax.ppermute(expn1, "layer", swap)
    *hops, block1 = call(
        outer_apply_kernel,
        (kept(points // CHUNKS, width),) * CHUNKS + (kept(*block),),
        diagonals,
        (source1,),
        [field, field],
        CHUNKS,
        **large,
    )
    arrived = [lax.ppermute(hop, "layer", swap) for hop in hops]
    basis1, mixed = call(
        inner_mix_kernel,
        (kept(3 * k, points), kept(k, 4 * k)),
        (),
        (block1, packed, own, expn1, other),
        [],
        1,
        **large,
    )
    (before,) = call(
        outer_couple_kernel, (kept(k, width),), (), (gathered, couple1, mixed), [], 1, **small
    )
    before = lax.ppermute(before, "layer", swap)
    (sums,) = call(
        inner_prepare_kernel,
        (kept(2 * k, width, of=F32),),
        (),
        (*arrived, source1, basis1),
        [field, field],
        1,
        **small,
    )
    (payload,) = call(
        inner_gather_kernel,
        (like(owners, 2 * k + k // 2, width),),
        (),
        (before, sums, mixed, packed),
        [(2 * k + k // 2, width)],
        1,
        **small,
    )
    half = owners // 2
    ends = [[g * owners + p * half + o for g in (0, layers - 1) for o in range(half)] for p in range(2)]
    groups = [[g * owners + o for o in range(owners)] for g in range(1, layers - 1)] + ends
    second = lax.all_to_all(payload, ("layer", "trace"), 0, 0, axis_index_groups=groups)
    product, one, source2 = call(
        inner_apply_kernel,
        (kept(*field), kept(*field), kept(*field)),
        (source_up, source_down, *diagonals, payload),
        (*arrived, before, other, source1),
        [block, field],
        CHUNKS + 1,
        **large,
    )
    crossed = lax.ppermute(product, ("layer", "trace"), pairs)
    (coupled,) = call(
        inner_couple_kernel,
        (kept(2 * k, width),),
        (),
        (gathered, second, packed, couple1),
        [(total, width), (total, width)],
        1,
        **small,
    )
    reached = lax.ppermute(coupled, "layer", across)
    lower, bases = call(
        settle_kernel,
        (kept(2, points // 2, points), kept(2 * k, points)),
        (expansion, *diagonals),
        (coupled, packed),
        [],
        2 + CHUNKS // 2,
        **large,
    )
    step = points // CHUNKS
    most, two, turned, rest, tail = call(
        inner_second_kernel,
        (
            *(kept(points - step, width), kept(*field), kept(*field)),
            *(kept(2, step, points), kept(step, width)),
        ),
        diagonals,
        (crossed, reached, source2, lower, bases),
        [field, (2, points // 2 - step, points)],
        CHUNKS + 1,
        **large,
    )
    (last,) = call(
        inner_rest_kernel, (kept(step, width),), (), (rest, two, turned, tail), [], 1, **small
    )
    arrived = [lax.ppermute(part, "layer", swap) for part in (most, last)]
    return call(
        last_kernel,
        (like(1, *field), like(1, *field)),
        (),
        (*arrived, one, two, source1, source2),
        [field],
        2,
        **small,
    )


def solution(mesh):
    shards = wave if mesh.shape["layer"] == ITERS + 1 else jacobi
    return jax.shard_map(
        shards,
        mesh=mesh,
        in_specs=(
            P("layer", "trace", None),
            P("layer", "trace", None),
            P("layer", None, "trace", None),
            P("layer", None, "trace", None),
            P("layer", None, None, "trace"),
            P("layer", None, None, "trace"),
            P("layer", None, None, "trace", None),
        ),
        out_specs=(P("layer", "trace", None), P("layer", "trace", None)),
        check_vma=False,
    )
```

```python
import jax
import jax.numpy as jnp
from jax import lax
from jax.experimental import pallas as pl
from jax.experimental.pallas import tpu as pltpu
from jax.sharding import PartitionSpec as P

ITERS = 3
BF16 = jnp.bfloat16
F32 = jnp.float32


def rotate(field):
    half = field.shape[-1] // 2
    return jnp.concatenate([-field[..., half:], field[..., :half]], axis=-1)


def dot(a, b):
    return jnp.dot(a, b, preferred_element_type=F32)


def shifted(value, axis, steps):
    count = lax.axis_size(axis)
    initial, last = (max(0, -steps), min(count, count - steps))
    return lax.ppermute(value, axis, [(source, source + steps) for source in range(initial, last)])


def jacobi(source_up, source_down, diag_up, diag_down, projection, expansion, coupling):
    sources = (source_up[0], source_down[0])
    blocks = (diag_up[0], diag_down[0])
    fields = sources
    for step in range(ITERS):
        coeffs = [dot(projection[0, d], fields[d]).astype(BF16) for d in range(2)]
        gathered = lax.all_gather(jnp.stack(coeffs), "trace", axis=1, tiled=True)
        arrived = []
        for d in range(2):
            coupled = dot(coupling[0, d, 0], gathered[d])
            coupled = (coupled + dot(coupling[0, d, 1], rotate(gathered[d]))).astype(BF16)
            result = dot(blocks[d][0], fields[d]) + dot(blocks[d][1], rotate(fields[d]))
            result = result + lax.dot_general(
                expansion[0, d], coupled, (((0,), (0,)), ((), ())), preferred_element_type=F32
            )
            arrived.append(shifted(result.astype(BF16), "layer", 1 - 2 * d))
        fields = tuple(
            (sources[d].astype(F32) + arrived[d].astype(F32)).astype(BF16) for d in range(2)
        )
    return fields[0][None], fields[1][None]


CHUNKS = 4
HBM = pl.BlockSpec(memory_space=pltpu.HBM)
VMEM = pl.BlockSpec(memory_space=pltpu.VMEM)


def call(body, outs, far, near, scratch, sems, flops=0, moved=0, aliases=None):
    kept = [isinstance(out, tuple) for out in outs]
    return pl.pallas_call(
        body,
        out_shape=tuple(pltpu.VMEM(*out) if keep else out for out, keep in zip(outs, kept)),
        in_specs=[HBM] * len(far) + [VMEM] * len(near),
        out_specs=tuple(VMEM if keep else HBM for keep in kept),
        scratch_shapes=[pltpu.VMEM(shape, BF16) for shape in scratch]
        + [pltpu.SemaphoreType.DMA((sems,))],
        input_output_aliases=aliases or {},
        cost_estimate=pl.CostEstimate(flops=flops, bytes_accessed=moved, transcendentals=0),
        compiler_params=pltpu.CompilerParams(vmem_limit_bytes=24 * 2**20),
    )(*far, *near)


def roles():
    layer, layers = lax.axis_index("layer"), lax.axis_size("layer")
    outer = jnp.logical_or(layer == 0, layer == layers - 1)
    return outer, jnp.where(layer >= layers // 2, 1, 0)


def start(source, target, sem):
    copy = pltpu.make_async_copy(source, target, sem)
    copy.start()
    return copy


def pick(which, up_ref, down_ref, target, sem):
    @pl.when(which == 0)
    def _():
        start(up_ref, target, sem)

    @pl.when(which != 0)
    def _():
        start(down_ref, target, sem)


def arrive(target, sem):
    pltpu.make_async_copy(target, target, sem).wait()


def chunk(c, size):
    step = size // CHUNKS
    return pl.ds(pl.multiple_of(c * step, step), step)


def each_chunk(size, body):
    def one(c, carry):
        body(c, chunk(c, size))
        return carry

    lax.fori_loop(0, CHUNKS, one, 0)


def load_block(which, up_ref, down_ref, block, sems, base):
    def one(c, rows):
        pick(
            which,
            up_ref.at[0, :, rows, :],
            down_ref.at[0, :, rows, :],
            block.at[:, rows, :],
            sems.at[base + c],
        )

    each_chunk(block.shape[1], one)


def block_rows(block, rows, field, turned):
    return dot(block[0, rows, :], field[...]) + dot(block[1, rows, :], turned[...])


def dot_rows(a, b):
    return lax.dot_general(a, b, (((1,), (1,)), ((), ())), preferred_element_type=F32)


def expand(basis, coupled):
    return lax.dot_general(basis, coupled, (((0,), (0,)), ((), ())), preferred_element_type=F32)


def first_kernel(
    sup, sdn, proj, expn, coup,
    payload, pack, source1, own, expn1, couple1,
    other, after, source2, coeffs, sems,
):
    outer, first = roles()
    second = 1 - first
    k, points, total = proj.shape[2], proj.shape[3], coup.shape[4]
    owners, width = payload.shape[0], source1.shape[1]
    start(coup.at[0, first], couple1, sems.at[0])
    start(proj.at[0, first], own, sems.at[1])
    pick(first, sup.at[0], sdn.at[0], source1, sems.at[2])
    start(expn.at[0, first], expn1, sems.at[3])

    @pl.when(outer)
    def _():
        arrive(own, sems.at[1])
        arrive(source1, sems.at[2])
        coeffs[...] = dot(own[...], source1[...]).astype(BF16)
        for o in range(owners):
            start(coeffs, payload.at[o, 0, :, pl.ds(0, width)], sems.at[4])
        arrive(couple1, sems.at[0])
        arrive(expn1, sems.at[3])
        arrive(payload.at[:, 0, :, pl.ds(0, width)], sems.at[4])

    @pl.when(jnp.logical_not(outer))
    def _():
        start(proj.at[0, second], other, sems.at[5])
        start(coup.at[0, second], after, sems.at[6])
        pick(second, sup.at[0], sdn.at[0], source2, sems.at[7])
        arrive(couple1, sems.at[0])
        for o in range(owners):
            start(couple1, payload.at[o, :, :, pl.ds(0, total)], sems.at[4])
        arrive(expn1, sems.at[3])
        arrive(other, sems.at[5])
        arrive(after, sems.at[6])
        pack[:k, :points] = other[...]
        pack[2 * k :, :points] = expn1[...]
        for part in range(2):
            pack[k : 2 * k, part * total : (part + 1) * total] = after[part]
        arrive(source2, sems.at[7])
        beyond = dot(other[...], source2[...]).astype(BF16)
        pack[k : 2 * k, 2 * total : 2 * total + width] = beyond
        arrive(own, sems.at[1])
        arrive(source1, sems.at[2])
        arrive(payload.at[:, :, :, pl.ds(0, total)], sems.at[4])


def outer_apply_kernel(dup, ddn, source1, *refs):
    hops, (block, turned, result, sems) = refs[:CHUNKS], refs[CHUNKS:]
    outer, first = roles()
    load_block(first, dup, ddn, block, sems, 0)

    @pl.when(outer)
    def _():
        step = source1.shape[0] // CHUNKS
        turned[...] = rotate(source1[...])

        def one(c, rows):
            arrive(block.at[:, rows, :], sems.at[c])
            result[rows, :] = block_rows(block, rows, source1, turned).astype(BF16)

        each_chunk(source1.shape[0], one)
        for c, hop in enumerate(hops):
            hop[...] = result[c * step : (c + 1) * step, :]

    @pl.when(jnp.logical_not(outer))
    def _():
        each_chunk(
            block.shape[1], lambda c, rows: arrive(block.at[:, rows, :], sems.at[c])
        )


def inner_mix_kernel(block, packed, own, expn1, before, basis, mixed, sems):
    del sems
    outer, _ = roles()

    @pl.when(jnp.logical_not(outer))
    def _():
        k, points = own.shape
        other = packed[:k, :points]
        mixed[:, :k] = dot_rows(other, expn1[...]).astype(BF16)
        step = points // CHUNKS
        parts = [0.0, 0.0]
        for c in range(CHUNKS):
            rows = pl.ds(c * step, step)
            for part in range(2):
                columns = other[:, c * step : (c + 1) * step]
                parts[part] = parts[part] + dot(columns, block[part, rows, :])
        basis[:k, :] = own[...]
        for part in range(2):
            basis[(1 + part) * k : (2 + part) * k, :] = parts[part].astype(BF16)
        value = dot_rows(basis[...], before[...]).astype(BF16)
        for part in range(3):
            mixed[:, (1 + part) * k : (2 + part) * k] = value[part * k : (part + 1) * k, :]


def inner_prepare_kernel(*refs):
    arrived, refs = refs[:CHUNKS], refs[CHUNKS:]
    source1, basis, sums, field, turned, sems = refs
    del sems
    outer, _ = roles()

    @pl.when(jnp.logical_not(outer))
    def _():
        k, points = basis.shape[0] // 3, basis.shape[1]
        step = points // CHUNKS
        for c, part in enumerate(arrived):
            rows = slice(c * step, (c + 1) * step)
            value = (source1[rows, :].astype(F32) + part[...].astype(F32)).astype(BF16)
            field[rows, :] = value
            turned[rows, :] = rotate(value)
        sums[...] = dot(basis[: 2 * k, :], field[...])
        sums[k:, :] += dot(basis[2 * k :, :], turned[...])


def outer_couple_kernel(gathered, couple1, mixed, out, sems):
    del mixed, sems
    outer, _ = roles()

    @pl.when(outer)
    def _():
        total = couple1.shape[2]
        coeffs = gathered[:, 0, :, : out.shape[1]].reshape(total, out.shape[1])
        out[...] = (dot(couple1[0], coeffs) + dot(couple1[1], rotate(coeffs))).astype(BF16)


def inner_gather_kernel(before, sums, mixed, packed, payload, small, sems):
    outer, _ = roles()

    @pl.when(jnp.logical_not(outer))
    def _():
        k, width = before.shape
        half, place = k // 2, 2 * k * payload.shape[0]
        coeffs = before[...]
        small[:k, :] = (sums[:k, :] + dot(mixed[:, k : 2 * k], coeffs)).astype(BF16)
        added = dot(mixed[:, 2 * k : 3 * k], coeffs)
        added = added + dot(mixed[:, 3 * k : 4 * k], rotate(coeffs))
        added = added + packed[k : 2 * k, place : place + width].astype(F32)
        small[k : 2 * k, :] = (sums[k:, :] + added).astype(BF16)
        small[2 * k :, :k] = mixed[:half, :k]
        small[2 * k :, k : 2 * k] = mixed[half:, :k]
        for o in range(payload.shape[0]):
            start(small, payload.at[o], sems.at[0])
        arrive(payload, sems.at[0])


def inner_apply_kernel(sup, sdn, dup, ddn, payload, *refs):
    del payload
    arrived, refs = refs[:CHUNKS], refs[CHUNKS:]
    before, other, source1, product, trace, source2, block, turned, sems = refs
    outer, first = roles()
    pick(1 - first, sup.at[0], sdn.at[0], source2, sems.at[CHUNKS])

    @pl.when(jnp.logical_not(outer))
    def _():
        load_block(first, dup, ddn, block, sems, 0)
        points = source1.shape[0]
        step = points // CHUNKS
        added = expand(other[...], before[...])
        for c, part in enumerate(arrived):
            rows = slice(c * step, (c + 1) * step)
            value = source1[rows, :].astype(F32) + part[...].astype(F32)
            value = (value + added[rows, :]).astype(BF16)
            trace[rows, :] = value
            turned[rows, :] = rotate(value)

        def one(c, rows):
            arrive(block.at[:, rows, :], sems.at[c])
            product[rows, :] = block_rows(block, rows, trace, turned).astype(BF16)

        each_chunk(points, one)

    arrive(source2, sems.at[CHUNKS])


def inner_couple_kernel(gathered, second, packed, couple1, out, inner, later, sems):
    del sems
    outer, _ = roles()

    @pl.when(jnp.logical_not(outer))
    def _():
        owners, width = second.shape[0], second.shape[2]
        k, total = couple1.shape[1:]
        coeffs = second[:, :k, :].reshape(total, width)
        turned = rotate(coeffs)
        real = gathered[:, 0, :, :total].reshape(total, total)
        imag = gathered[:, 1, :, :total].reshape(total, total)
        inner[...] = (dot(real, coeffs) + dot(imag, turned)).astype(BF16)
        out[:k, :] = (dot(couple1[0], coeffs) + dot(couple1[1], turned)).astype(BF16)
        for o in range(owners):
            rows = slice(o * k, (o + 1) * k)
            own = inner[rows, :]
            added = [dot(second[o, 2 * k :, h * k : (h + 1) * k], own) for h in range(2)]
            added = jnp.concatenate(added, axis=0)
            later[rows, :] = (second[o, k : 2 * k, :].astype(F32) + added).astype(BF16)
        coeffs = later[...]
        result = dot(packed[k : 2 * k, :total], coeffs)
        result = result + dot(packed[k : 2 * k, total : 2 * total], rotate(coeffs))
        out[k:, :] = result.astype(BF16)


def load_part(first_chunk, which, up_ref, down_ref, block, size, sems, base):
    for c in range(block.shape[1] // size):
        source = pl.ds((first_chunk + c) * size, size)
        pick(
            which,
            up_ref.at[0, :, source, :],
            down_ref.at[0, :, source, :],
            block.at[:, pl.ds(c * size, size), :],
            sems.at[base + c],
        )


def each_chunk_of(block, size, body):
    def one(c, carry):
        body(c, pl.ds(pl.multiple_of(c * size, size), size))
        return carry

    lax.fori_loop(0, block.shape[1] // size, one, 0)


def put(which, source, up, down, sem):
    @pl.when(which == 0)
    def _():
        start(source, up.at[0], sem)

    @pl.when(which != 0)
    def _():
        start(source, down.at[0], sem)


def settle_kernel(
    expn, dup, ddn, coupled, packed, lower, bases, sems
):
    del coupled
    outer, first = roles()

    @pl.when(jnp.logical_not(outer))
    def _():
        k, points = bases.shape[0] // 2, bases.shape[1]
        start(expn.at[0, 1 - first], bases.at[pl.ds(k, k), :], sems.at[1])
        step = points // CHUNKS
        load_part(0, 1 - first, dup, ddn, lower, step, sems, 2)
        bases[:k, :] = packed[2 * k :, :points]
        arrive(bases.at[pl.ds(k, k), :], sems.at[1])
        each_chunk_of(
            lower, step, lambda c, rows: arrive(lower.at[:, rows, :], sems.at[2 + c])
        )


def inner_second_kernel(
    dup, ddn, crossed, coupled, source2, lower, bases, source1, one,
    up, down, out, trace, turned, rest, tail, added2, upper, sems,
):
    outer, first = roles()

    @pl.when(outer)
    def _():
        put(first, source1, up, down, sems.at[CHUNKS + 1])

    @pl.when(jnp.logical_not(outer))
    def _():
        put(first, one, up, down, sems.at[CHUNKS + 1])

    @pl.when(jnp.logical_not(outer))
    def _():
        k, points = coupled.shape[0] // 2, bases.shape[1]
        step = points // CHUNKS
        load_part(CHUNKS // 2, 1 - first, dup, ddn, upper, step, sems, 0)
        load_part(CHUNKS - 1, 1 - first, dup, ddn, rest, step, sems, CHUNKS)

        added = expand(bases[:k, :], coupled[:k, :])
        for c in range(CHUNKS):
            rows = slice(c * step, (c + 1) * step)
            value = source2[rows, :].astype(F32) + crossed[rows, :].astype(F32)
            value = (value + added[rows, :]).astype(BF16)
            trace[rows, :] = value
            turned[rows, :] = rotate(value)
        added2[...] = expand(bases[k:, :], coupled[k:, :]).astype(BF16)
        tail[...] = added2[points - step :, :]

        def put(block, rows, base):
            place = pl.ds(pl.multiple_of(rows.start + base, step), step)
            value = block_rows(block, rows, trace, turned) + added2[place, :].astype(F32)
            out[place, :] = value.astype(BF16)

        each_chunk_of(lower, step, lambda c, rows: put(lower, rows, 0))

        def second(c, rows):
            arrive(upper.at[:, rows, :], sems.at[c])
            put(upper, rows, points // 2)

        each_chunk_of(upper, step, second)
        arrive(rest, sems.at[CHUNKS])

    arrive(source1, sems.at[CHUNKS + 1])


def inner_rest_kernel(rest, trace, turned, tail, out, sems):
    del sems
    outer, _ = roles()

    @pl.when(jnp.logical_not(outer))
    def _():
        value = dot(rest[0], trace[...]) + dot(rest[1], turned[...])
        out[...] = (value + tail[...].astype(F32)).astype(BF16)


def last_kernel(before_up, before_down, most, last, two, source2, up, down, sums, sems):
    del before_up, before_down
    outer, first = roles()

    def put_rows(which, rows, sem):
        @pl.when(which == 0)
        def _():
            start(sums.at[rows, :], up.at[0, rows, :], sem)

        @pl.when(which != 0)
        def _():
            start(sums.at[rows, :], down.at[0, rows, :], sem)

    @pl.when(outer)
    def _():
        cut = most.shape[0]
        for part, rows in ((most, pl.ds(0, cut)), (last, pl.ds(cut, sums.shape[0] - cut))):
            value = source2[rows, :].astype(F32) + part[...].astype(F32)
            sums[rows, :] = value.astype(BF16)
            put_rows(1 - first, rows, sems.at[0])

    @pl.when(jnp.logical_not(outer))
    def _():
        put(1 - first, two, up, down, sems.at[0])

    arrive(sums, sems.at[0])


def wave(*arrays):
    layers, owners = lax.axis_size("layer"), lax.axis_size("trace")
    source_up, source_down, diag_up, diag_down, projection, expansion, coupling = (
        pltpu.with_memory_space_constraint(array, pltpu.HBM) for array in arrays
    )
    _, points, width = source_up.shape
    k, total = projection.shape[2], coupling.shape[4]
    swap = [(g, g ^ 1) for g in range(layers)]
    across = [(g, layers - 1 - g) for g in range(layers)]
    inside = across[1:-1]

    def like(*shape):
        return jax.ShapeDtypeStruct(shape, BF16)

    def kept(*shape, of=BF16):
        return shape, of

    field, block, basis, couple = (points, width), (2, points, points), (k, points), (2, k, total)
    small = dict(flops=2 * k * points * width, moved=4 * points * width)
    large = dict(flops=4 * points * points * width, moved=4 * points * points)
    diagonals = (diag_up, diag_down)
    packing = max(points, 2 * total + width)

    payload, pack, source1, own, expn1, couple1 = call(
        first_kernel,
        (
            like(owners, 2, k, max(total, width)),
            *(kept(3 * k, packing), kept(*field), kept(*basis), kept(*basis), kept(*couple)),
        ),
        (source_up, source_down, projection, expansion, coupling),
        (),
        [basis, couple, field, (k, width)],
        8,
        **small,
    )
    gathered = lax.all_to_all(payload, "trace", 0, 0)
    pairs = [(a * owners + o, b * owners + o) for a, b in inside for o in range(owners)]
    pairs += [(g * owners + o, g * owners + (o ^ 1)) for g in (0, layers - 1) for o in range(owners)]
    packed = lax.ppermute(pack, ("layer", "trace"), pairs)
    other = lax.ppermute(expn1, "layer", swap)
    *hops, block1 = call(
        outer_apply_kernel,
        (kept(points // CHUNKS, width),) * CHUNKS + (kept(*block),),
        diagonals,
        (source1,),
        [field, field],
        CHUNKS,
        **large,
    )
    arrived = [lax.ppermute(hop, "layer", swap) for hop in hops]
    basis1, mixed = call(
        inner_mix_kernel,
        (kept(3 * k, points), kept(k, 4 * k)),
        (),
        (block1, packed, own, expn1, other),
        [],
        1,
        **large,
    )
    (before,) = call(
        outer_couple_kernel, (kept(k, width),), (), (gathered, couple1, mixed), [], 1, **small
    )
    before = lax.ppermute(before, "layer", swap)
    (sums,) = call(
        inner_prepare_kernel,
        (kept(2 * k, width, of=F32),),
        (),
        (*arrived, source1, basis1),
        [field, field],
        1,
        **small,
    )
    (payload,) = call(
        inner_gather_kernel,
        (like(owners, 2 * k + k // 2, width),),
        (),
        (before, sums, mixed, packed),
        [(2 * k + k // 2, width)],
        1,
        **small,
    )
    half = owners // 2
    ends = [[g * owners + p * half + o for g in (0, layers - 1) for o in range(half)] for p in range(2)]
    groups = [[g * owners + o for o in range(owners)] for g in range(1, layers - 1)] + ends
    second = lax.all_to_all(payload, ("layer", "trace"), 0, 0, axis_index_groups=groups)
    product, one, source2 = call(
        inner_apply_kernel,
        (kept(*field), kept(*field), kept(*field)),
        (source_up, source_down, *diagonals, payload),
        (*arrived, before, other, source1),
        [block, field],
        CHUNKS + 1,
        **large,
    )
    crossed = lax.ppermute(product, ("layer", "trace"), pairs)
    (coupled,) = call(
        inner_couple_kernel,
        (kept(2 * k, width),),
        (),
        (gathered, second, packed, couple1),
        [(total, width), (total, width)],
        1,
        **small,
    )
    reached = lax.ppermute(coupled, "layer", across)
    lower, bases = call(
        settle_kernel,
        (kept(2, points // 2, points), kept(2 * k, points)),
        (expansion, *diagonals),
        (coupled, packed),
        [],
        2 + CHUNKS // 2,
        **large,
    )
    step = points // CHUNKS
    up, down, most, two, turned, rest, tail = call(
        inner_second_kernel,
        (
            *(like(1, *field), like(1, *field)),
            *(kept(points - step, width), kept(*field), kept(*field)),
            *(kept(2, step, points), kept(step, width)),
        ),
        diagonals,
        (crossed, reached, source2, lower, bases, source1, one),
        [field, (2, points // 2 - step, points)],
        CHUNKS + 2,
        **large,
    )
    (last,) = call(
        inner_rest_kernel, (kept(step, width),), (), (rest, two, turned, tail), [], 1, **small
    )
    arrived = [lax.ppermute(part, "layer", swap) for part in (most, last)]
    return call(
        last_kernel,
        (like(1, *field), like(1, *field)),
        (up, down),
        (*arrived, two, source2),
        [field],
        1,
        aliases={0: 0, 1: 1},
        **small,
    )


def solution(mesh):
    shards = wave if mesh.shape["layer"] == ITERS + 1 else jacobi
    return jax.shard_map(
        shards,
        mesh=mesh,
        in_specs=(
            P("layer", "trace", None),
            P("layer", "trace", None),
            P("layer", None, "trace", None),
            P("layer", None, "trace", None),
            P("layer", None, None, "trace"),
            P("layer", None, None, "trace"),
            P("layer", None, None, "trace", None),
        ),
        out_specs=(P("layer", "trace", None), P("layer", "trace", None)),
        check_vma=False,
    )
```

```python
import jax
import jax.numpy as jnp
from jax import lax
from jax.experimental import pallas as pl
from jax.experimental.pallas import tpu as pltpu
from jax.sharding import PartitionSpec as P

ITERS = 3
BF16 = jnp.bfloat16
F32 = jnp.float32


def rotate(field):
    half = field.shape[-1] // 2
    return jnp.concatenate([-field[..., half:], field[..., :half]], axis=-1)


def dot(a, b):
    return jnp.dot(a, b, preferred_element_type=F32)


def shifted(value, axis, steps):
    count = lax.axis_size(axis)
    initial, last = (max(0, -steps), min(count, count - steps))
    return lax.ppermute(value, axis, [(source, source + steps) for source in range(initial, last)])


def jacobi(source_up, source_down, diag_up, diag_down, projection, expansion, coupling):
    sources = (source_up[0], source_down[0])
    blocks = (diag_up[0], diag_down[0])
    fields = sources
    for step in range(ITERS):
        coeffs = [dot(projection[0, d], fields[d]).astype(BF16) for d in range(2)]
        gathered = lax.all_gather(jnp.stack(coeffs), "trace", axis=1, tiled=True)
        arrived = []
        for d in range(2):
            coupled = dot(coupling[0, d, 0], gathered[d])
            coupled = (coupled + dot(coupling[0, d, 1], rotate(gathered[d]))).astype(BF16)
            result = dot(blocks[d][0], fields[d]) + dot(blocks[d][1], rotate(fields[d]))
            result = result + lax.dot_general(
                expansion[0, d], coupled, (((0,), (0,)), ((), ())), preferred_element_type=F32
            )
            arrived.append(shifted(result.astype(BF16), "layer", 1 - 2 * d))
        fields = tuple(
            (sources[d].astype(F32) + arrived[d].astype(F32)).astype(BF16) for d in range(2)
        )
    return fields[0][None], fields[1][None]


CHUNKS = 4
HBM = pl.BlockSpec(memory_space=pltpu.HBM)
VMEM = pl.BlockSpec(memory_space=pltpu.VMEM)


def call(body, outs, far, near, scratch, sems, flops=0, moved=0, aliases=None):
    kept = [isinstance(out, tuple) for out in outs]
    return pl.pallas_call(
        body,
        out_shape=tuple(pltpu.VMEM(*out) if keep else out for out, keep in zip(outs, kept)),
        in_specs=[HBM] * len(far) + [VMEM] * len(near),
        out_specs=tuple(VMEM if keep else HBM for keep in kept),
        scratch_shapes=[pltpu.VMEM(shape, BF16) for shape in scratch]
        + [pltpu.SemaphoreType.DMA((sems,))],
        input_output_aliases=aliases or {},
        cost_estimate=pl.CostEstimate(flops=flops, bytes_accessed=moved, transcendentals=0),
        compiler_params=pltpu.CompilerParams(vmem_limit_bytes=24 * 2**20),
    )(*far, *near)


def roles():
    layer, layers = lax.axis_index("layer"), lax.axis_size("layer")
    outer = jnp.logical_or(layer == 0, layer == layers - 1)
    return outer, jnp.where(layer >= layers // 2, 1, 0)


def start(source, target, sem):
    copy = pltpu.make_async_copy(source, target, sem)
    copy.start()
    return copy


def pick(which, up_ref, down_ref, target, sem):
    @pl.when(which == 0)
    def _():
        start(up_ref, target, sem)

    @pl.when(which != 0)
    def _():
        start(down_ref, target, sem)


def arrive(target, sem):
    pltpu.make_async_copy(target, target, sem).wait()


def chunk(c, size):
    step = size // CHUNKS
    return pl.ds(pl.multiple_of(c * step, step), step)


def each_chunk(size, body):
    def one(c, carry):
        body(c, chunk(c, size))
        return carry

    lax.fori_loop(0, CHUNKS, one, 0)


def load_block(which, up_ref, down_ref, block, sems, base):
    def one(c, rows):
        pick(
            which,
            up_ref.at[0, :, rows, :],
            down_ref.at[0, :, rows, :],
            block.at[:, rows, :],
            sems.at[base + c],
        )

    each_chunk(block.shape[1], one)


def block_rows(block, rows, field, turned):
    return dot(block[0, rows, :], field[...]) + dot(block[1, rows, :], turned[...])


def dot_rows(a, b):
    return lax.dot_general(a, b, (((1,), (1,)), ((), ())), preferred_element_type=F32)


def expand(basis, coupled):
    return lax.dot_general(basis, coupled, (((0,), (0,)), ((), ())), preferred_element_type=F32)


def first_kernel(
    sup, sdn, proj, expn, coup,
    payload, pack, source1, own, expn1, couple1,
    other, after, source2, coeffs, sems,
):
    outer, first = roles()
    second = 1 - first
    k, points, total = proj.shape[2], proj.shape[3], coup.shape[4]
    owners, width = payload.shape[0], source1.shape[1]
    start(coup.at[0, first], couple1, sems.at[0])
    start(proj.at[0, first], own, sems.at[1])
    pick(first, sup.at[0], sdn.at[0], source1, sems.at[2])
    start(expn.at[0, first], expn1, sems.at[3])

    @pl.when(outer)
    def _():
        arrive(own, sems.at[1])
        arrive(source1, sems.at[2])
        coeffs[...] = dot(own[...], source1[...]).astype(BF16)
        for o in range(owners):
            start(coeffs, payload.at[o, 0, :, pl.ds(0, width)], sems.at[4])
        arrive(couple1, sems.at[0])
        arrive(expn1, sems.at[3])
        arrive(payload.at[:, 0, :, pl.ds(0, width)], sems.at[4])

    @pl.when(jnp.logical_not(outer))
    def _():
        start(proj.at[0, second], other, sems.at[5])
        start(coup.at[0, second], after, sems.at[6])
        pick(second, sup.at[0], sdn.at[0], source2, sems.at[7])
        arrive(couple1, sems.at[0])
        for o in range(owners):
            start(couple1, payload.at[o, :, :, pl.ds(0, total)], sems.at[4])
        arrive(expn1, sems.at[3])
        arrive(other, sems.at[5])
        arrive(after, sems.at[6])
        pack[:k, :points] = other[...]
        pack[2 * k :, :points] = expn1[...]
        for part in range(2):
            pack[k : 2 * k, part * total : (part + 1) * total] = after[part]
        arrive(source2, sems.at[7])
        beyond = dot(other[...], source2[...]).astype(BF16)
        pack[k : 2 * k, 2 * total : 2 * total + width] = beyond
        arrive(own, sems.at[1])
        arrive(source1, sems.at[2])
        arrive(payload.at[:, :, :, pl.ds(0, total)], sems.at[4])


def outer_apply_kernel(dup, ddn, source1, *refs):
    hops, (block, turned, result, sems) = refs[:CHUNKS], refs[CHUNKS:]
    outer, first = roles()
    load_block(first, dup, ddn, block, sems, 0)

    @pl.when(outer)
    def _():
        step = source1.shape[0] // CHUNKS
        turned[...] = rotate(source1[...])

        def one(c, rows):
            arrive(block.at[:, rows, :], sems.at[c])
            result[rows, :] = block_rows(block, rows, source1, turned).astype(BF16)

        each_chunk(source1.shape[0], one)
        for c, hop in enumerate(hops):
            hop[...] = result[c * step : (c + 1) * step, :]

    @pl.when(jnp.logical_not(outer))
    def _():
        each_chunk(
            block.shape[1], lambda c, rows: arrive(block.at[:, rows, :], sems.at[c])
        )


def inner_mix_kernel(block, packed, own, expn1, before, basis, mixed, sems):
    del sems
    outer, _ = roles()

    @pl.when(jnp.logical_not(outer))
    def _():
        k, points = own.shape
        other = packed[:k, :points]
        mixed[:, :k] = dot_rows(other, expn1[...]).astype(BF16)
        step = points // CHUNKS
        parts = [0.0, 0.0]
        for c in range(CHUNKS):
            rows = pl.ds(c * step, step)
            for part in range(2):
                columns = other[:, c * step : (c + 1) * step]
                parts[part] = parts[part] + dot(columns, block[part, rows, :])
        basis[:k, :] = own[...]
        for part in range(2):
            basis[(1 + part) * k : (2 + part) * k, :] = parts[part].astype(BF16)
        value = dot_rows(basis[...], before[...]).astype(BF16)
        for part in range(3):
            mixed[:, (1 + part) * k : (2 + part) * k] = value[part * k : (part + 1) * k, :]


def inner_prepare_kernel(*refs):
    arrived, refs = refs[:CHUNKS], refs[CHUNKS:]
    source1, basis, sums, field, turned, sems = refs
    del sems
    outer, _ = roles()

    @pl.when(jnp.logical_not(outer))
    def _():
        k, points = basis.shape[0] // 3, basis.shape[1]
        step = points // CHUNKS
        for c, part in enumerate(arrived):
            rows = slice(c * step, (c + 1) * step)
            value = (source1[rows, :].astype(F32) + part[...].astype(F32)).astype(BF16)
            field[rows, :] = value
            turned[rows, :] = rotate(value)
        sums[...] = dot(basis[: 2 * k, :], field[...])
        sums[k:, :] += dot(basis[2 * k :, :], turned[...])


def outer_couple_kernel(gathered, couple1, mixed, out, sems):
    del mixed, sems
    outer, _ = roles()

    @pl.when(outer)
    def _():
        total = couple1.shape[2]
        coeffs = gathered[:, 0, :, : out.shape[1]].reshape(total, out.shape[1])
        out[...] = (dot(couple1[0], coeffs) + dot(couple1[1], rotate(coeffs))).astype(BF16)


def inner_gather_kernel(before, sums, mixed, packed, payload, small, sems):
    outer, _ = roles()

    @pl.when(jnp.logical_not(outer))
    def _():
        k, width = before.shape
        half, place = k // 2, 2 * k * payload.shape[0]
        coeffs = before[...]
        small[:k, :] = (sums[:k, :] + dot(mixed[:, k : 2 * k], coeffs)).astype(BF16)
        added = dot(mixed[:, 2 * k : 3 * k], coeffs)
        added = added + dot(mixed[:, 3 * k : 4 * k], rotate(coeffs))
        added = added + packed[k : 2 * k, place : place + width].astype(F32)
        small[k : 2 * k, :] = (sums[k:, :] + added).astype(BF16)
        small[2 * k :, :k] = mixed[:half, :k]
        small[2 * k :, k : 2 * k] = mixed[half:, :k]
        for o in range(payload.shape[0]):
            start(small, payload.at[o], sems.at[0])
        arrive(payload, sems.at[0])


def inner_apply_kernel(sup, sdn, dup, ddn, payload, *refs):
    del payload
    arrived, refs = refs[:CHUNKS], refs[CHUNKS:]
    before, other, source1, product, trace, source2, block, turned, sems = refs
    outer, first = roles()
    pick(1 - first, sup.at[0], sdn.at[0], source2, sems.at[CHUNKS])

    @pl.when(jnp.logical_not(outer))
    def _():
        load_block(first, dup, ddn, block, sems, 0)
        points = source1.shape[0]
        step = points // CHUNKS
        added = expand(other[...], before[...])
        for c, part in enumerate(arrived):
            rows = slice(c * step, (c + 1) * step)
            value = source1[rows, :].astype(F32) + part[...].astype(F32)
            value = (value + added[rows, :]).astype(BF16)
            trace[rows, :] = value
            turned[rows, :] = rotate(value)

        def one(c, rows):
            arrive(block.at[:, rows, :], sems.at[c])
            product[rows, :] = block_rows(block, rows, trace, turned).astype(BF16)

        each_chunk(points, one)

    arrive(source2, sems.at[CHUNKS])


def inner_couple_kernel(gathered, second, packed, couple1, out, inner, later, sems):
    del sems
    outer, _ = roles()

    @pl.when(jnp.logical_not(outer))
    def _():
        owners, width = second.shape[0], second.shape[2]
        k, total = couple1.shape[1:]
        coeffs = second[:, :k, :].reshape(total, width)
        turned = rotate(coeffs)
        real = gathered[:, 0, :, :total].reshape(total, total)
        imag = gathered[:, 1, :, :total].reshape(total, total)
        inner[...] = (dot(real, coeffs) + dot(imag, turned)).astype(BF16)
        out[:k, :] = (dot(couple1[0], coeffs) + dot(couple1[1], turned)).astype(BF16)
        for o in range(owners):
            rows = slice(o * k, (o + 1) * k)
            own = inner[rows, :]
            added = [dot(second[o, 2 * k :, h * k : (h + 1) * k], own) for h in range(2)]
            added = jnp.concatenate(added, axis=0)
            later[rows, :] = (second[o, k : 2 * k, :].astype(F32) + added).astype(BF16)
        coeffs = later[...]
        result = dot(packed[k : 2 * k, :total], coeffs)
        result = result + dot(packed[k : 2 * k, total : 2 * total], rotate(coeffs))
        out[k:, :] = result.astype(BF16)


def load_part(first_chunk, which, up_ref, down_ref, block, size, sems, base):
    for c in range(block.shape[1] // size):
        source = pl.ds((first_chunk + c) * size, size)
        pick(
            which,
            up_ref.at[0, :, source, :],
            down_ref.at[0, :, source, :],
            block.at[:, pl.ds(c * size, size), :],
            sems.at[base + c],
        )


def each_chunk_of(block, size, body):
    def one(c, carry):
        body(c, pl.ds(pl.multiple_of(c * size, size), size))
        return carry

    lax.fori_loop(0, block.shape[1] // size, one, 0)


def put(which, source, up, down, sem):
    @pl.when(which == 0)
    def _():
        start(source, up.at[0], sem)

    @pl.when(which != 0)
    def _():
        start(source, down.at[0], sem)


def settle_kernel(
    expn, dup, ddn, coupled, packed, source1, one, up, down, lower, bases, sems
):
    del coupled
    outer, first = roles()

    @pl.when(outer)
    def _():
        put(first, source1, up, down, sems.at[0])

    @pl.when(jnp.logical_not(outer))
    def _():
        put(first, one, up, down, sems.at[0])

    @pl.when(jnp.logical_not(outer))
    def _():
        k, points = bases.shape[0] // 2, bases.shape[1]
        start(expn.at[0, 1 - first], bases.at[pl.ds(k, k), :], sems.at[1])
        step = points // CHUNKS
        load_part(0, 1 - first, dup, ddn, lower, step, sems, 2)
        bases[:k, :] = packed[2 * k :, :points]
        arrive(bases.at[pl.ds(k, k), :], sems.at[1])
        each_chunk_of(
            lower, step, lambda c, rows: arrive(lower.at[:, rows, :], sems.at[2 + c])
        )

    arrive(source1, sems.at[0])


def inner_second_kernel(
    dup, ddn, crossed, coupled, source2, lower, bases,
    out, trace, turned, rest, tail, added2, upper, sems,
):
    outer, first = roles()

    @pl.when(jnp.logical_not(outer))
    def _():
        k, points = coupled.shape[0] // 2, bases.shape[1]
        step = points // CHUNKS
        load_part(CHUNKS // 2, 1 - first, dup, ddn, upper, step, sems, 0)
        load_part(CHUNKS - 1, 1 - first, dup, ddn, rest, step, sems, CHUNKS)

        added = expand(bases[:k, :], coupled[:k, :])
        for c in range(CHUNKS):
            rows = slice(c * step, (c + 1) * step)
            value = source2[rows, :].astype(F32) + crossed[rows, :].astype(F32)
            value = (value + added[rows, :]).astype(BF16)
            trace[rows, :] = value
            turned[rows, :] = rotate(value)
        added2[...] = expand(bases[k:, :], coupled[k:, :]).astype(BF16)
        tail[...] = added2[points - step :, :]

        def put(block, rows, base):
            place = pl.ds(pl.multiple_of(rows.start + base, step), step)
            value = block_rows(block, rows, trace, turned) + added2[place, :].astype(F32)
            out[place, :] = value.astype(BF16)

        each_chunk_of(lower, step, lambda c, rows: put(lower, rows, 0))

        def second(c, rows):
            arrive(upper.at[:, rows, :], sems.at[c])
            put(upper, rows, points // 2)

        each_chunk_of(upper, step, second)
        arrive(rest, sems.at[CHUNKS])


def inner_rest_kernel(rest, trace, turned, tail, out, sems):
    del sems
    outer, _ = roles()

    @pl.when(jnp.logical_not(outer))
    def _():
        value = dot(rest[0], trace[...]) + dot(rest[1], turned[...])
        out[...] = (value + tail[...].astype(F32)).astype(BF16)


def last_kernel(before_up, before_down, most, last, two, source2, up, down, sums, sems):
    del before_up, before_down
    outer, first = roles()

    def put_rows(which, rows, sem):
        @pl.when(which == 0)
        def _():
            start(sums.at[rows, :], up.at[0, rows, :], sem)

        @pl.when(which != 0)
        def _():
            start(sums.at[rows, :], down.at[0, rows, :], sem)

    @pl.when(outer)
    def _():
        cut = most.shape[0]
        for part, rows in ((most, pl.ds(0, cut)), (last, pl.ds(cut, sums.shape[0] - cut))):
            value = source2[rows, :].astype(F32) + part[...].astype(F32)
            sums[rows, :] = value.astype(BF16)
            put_rows(1 - first, rows, sems.at[0])

    @pl.when(jnp.logical_not(outer))
    def _():
        put(1 - first, two, up, down, sems.at[0])

    arrive(sums, sems.at[0])


def wave(*arrays):
    layers, owners = lax.axis_size("layer"), lax.axis_size("trace")
    source_up, source_down, diag_up, diag_down, projection, expansion, coupling = (
        pltpu.with_memory_space_constraint(array, pltpu.HBM) for array in arrays
    )
    _, points, width = source_up.shape
    k, total = projection.shape[2], coupling.shape[4]
    swap = [(g, g ^ 1) for g in range(layers)]
    across = [(g, layers - 1 - g) for g in range(layers)]
    inside = across[1:-1]

    def like(*shape):
        return jax.ShapeDtypeStruct(shape, BF16)

    def kept(*shape, of=BF16):
        return shape, of

    field, block, basis, couple = (points, width), (2, points, points), (k, points), (2, k, total)
    small = dict(flops=2 * k * points * width, moved=4 * points * width)
    large = dict(flops=4 * points * points * width, moved=4 * points * points)
    diagonals = (diag_up, diag_down)
    packing = max(points, 2 * total + width)

    payload, pack, source1, own, expn1, couple1 = call(
        first_kernel,
        (
            like(owners, 2, k, max(total, width)),
            *(kept(3 * k, packing), kept(*field), kept(*basis), kept(*basis), kept(*couple)),
        ),
        (source_up, source_down, projection, expansion, coupling),
        (),
        [basis, couple, field, (k, width)],
        8,
        **small,
    )
    gathered = lax.all_to_all(payload, "trace", 0, 0)
    pairs = [(a * owners + o, b * owners + o) for a, b in inside for o in range(owners)]
    pairs += [(g * owners + o, g * owners + (o ^ 1)) for g in (0, layers - 1) for o in range(owners)]
    packed = lax.ppermute(pack, ("layer", "trace"), pairs)
    other = lax.ppermute(expn1, "layer", swap)
    *hops, block1 = call(
        outer_apply_kernel,
        (kept(points // CHUNKS, width),) * CHUNKS + (kept(*block),),
        diagonals,
        (source1,),
        [field, field],
        CHUNKS,
        **large,
    )
    arrived = [lax.ppermute(hop, "layer", swap) for hop in hops]
    basis1, mixed = call(
        inner_mix_kernel,
        (kept(3 * k, points), kept(k, 4 * k)),
        (),
        (block1, packed, own, expn1, other),
        [],
        1,
        **large,
    )
    (before,) = call(
        outer_couple_kernel, (kept(k, width),), (), (gathered, couple1, mixed), [], 1, **small
    )
    before = lax.ppermute(before, "layer", swap)
    (sums,) = call(
        inner_prepare_kernel,
        (kept(2 * k, width, of=F32),),
        (),
        (*arrived, source1, basis1),
        [field, field],
        1,
        **small,
    )
    (payload,) = call(
        inner_gather_kernel,
        (like(owners, 2 * k + k // 2, width),),
        (),
        (before, sums, mixed, packed),
        [(2 * k + k // 2, width)],
        1,
        **small,
    )
    half = owners // 2
    ends = [[g * owners + p * half + o for g in (0, layers - 1) for o in range(half)] for p in range(2)]
    groups = [[g * owners + o for o in range(owners)] for g in range(1, layers - 1)] + ends
    second = lax.all_to_all(payload, ("layer", "trace"), 0, 0, axis_index_groups=groups)
    product, one, source2 = call(
        inner_apply_kernel,
        (kept(*field), kept(*field), kept(*field)),
        (source_up, source_down, *diagonals, payload),
        (*arrived, before, other, source1),
        [block, field],
        CHUNKS + 1,
        **large,
    )
    crossed = lax.ppermute(product, ("layer", "trace"), pairs)
    (coupled,) = call(
        inner_couple_kernel,
        (kept(2 * k, width),),
        (),
        (gathered, second, packed, couple1),
        [(total, width), (total, width)],
        1,
        **small,
    )
    reached = lax.ppermute(coupled, "layer", across)
    up, down, lower, bases = call(
        settle_kernel,
        (like(1, *field), like(1, *field), kept(2, points // 2, points), kept(2 * k, points)),
        (expansion, *diagonals),
        (coupled, packed, source1, one),
        [],
        2 + CHUNKS // 2,
        **large,
    )
    step = points // CHUNKS
    most, two, turned, rest, tail = call(
        inner_second_kernel,
        (
            *(kept(points - step, width), kept(*field), kept(*field)),
            *(kept(2, step, points), kept(step, width)),
        ),
        diagonals,
        (crossed, reached, source2, lower, bases),
        [field, (2, points // 2 - step, points)],
        CHUNKS + 1,
        **large,
    )
    (last,) = call(
        inner_rest_kernel, (kept(step, width),), (), (rest, two, turned, tail), [], 1, **small
    )
    arrived = [lax.ppermute(part, "layer", swap) for part in (most, last)]
    return call(
        last_kernel,
        (like(1, *field), like(1, *field)),
        (up, down),
        (*arrived, two, source2),
        [field],
        1,
        aliases={0: 0, 1: 1},
        **small,
    )


def solution(mesh):
    shards = wave if mesh.shape["layer"] == ITERS + 1 else jacobi
    return jax.shard_map(
        shards,
        mesh=mesh,
        in_specs=(
            P("layer", "trace", None),
            P("layer", "trace", None),
            P("layer", None, "trace", None),
            P("layer", None, "trace", None),
            P("layer", None, None, "trace"),
            P("layer", None, None, "trace"),
            P("layer", None, None, "trace", None),
        ),
        out_specs=(P("layer", "trace", None), P("layer", "trace", None)),
        check_vma=False,
    )
```

```python
import jax
import jax.numpy as jnp
from jax import lax
from jax.experimental import pallas as pl
from jax.experimental.pallas import tpu as pltpu
from jax.sharding import PartitionSpec as P

ITERS = 3
BF16 = jnp.bfloat16
F32 = jnp.float32


def rotate(field):
    half = field.shape[-1] // 2
    return jnp.concatenate([-field[..., half:], field[..., :half]], axis=-1)


def dot(a, b):
    return jnp.dot(a, b, preferred_element_type=F32)


def shifted(value, axis, steps):
    count = lax.axis_size(axis)
    initial, last = (max(0, -steps), min(count, count - steps))
    return lax.ppermute(value, axis, [(source, source + steps) for source in range(initial, last)])


def jacobi(source_up, source_down, diag_up, diag_down, projection, expansion, coupling):
    sources = (source_up[0], source_down[0])
    blocks = (diag_up[0], diag_down[0])
    fields = sources
    for step in range(ITERS):
        coeffs = [dot(projection[0, d], fields[d]).astype(BF16) for d in range(2)]
        gathered = lax.all_gather(jnp.stack(coeffs), "trace", axis=1, tiled=True)
        arrived = []
        for d in range(2):
            coupled = dot(coupling[0, d, 0], gathered[d])
            coupled = (coupled + dot(coupling[0, d, 1], rotate(gathered[d]))).astype(BF16)
            result = dot(blocks[d][0], fields[d]) + dot(blocks[d][1], rotate(fields[d]))
            result = result + lax.dot_general(
                expansion[0, d], coupled, (((0,), (0,)), ((), ())), preferred_element_type=F32
            )
            arrived.append(shifted(result.astype(BF16), "layer", 1 - 2 * d))
        fields = tuple(
            (sources[d].astype(F32) + arrived[d].astype(F32)).astype(BF16) for d in range(2)
        )
    return fields[0][None], fields[1][None]


CHUNKS = 4
HBM = pl.BlockSpec(memory_space=pltpu.HBM)
VMEM = pl.BlockSpec(memory_space=pltpu.VMEM)


def call(body, outs, far, near, scratch, sems, flops=0, moved=0, aliases=None):
    kept = [isinstance(out, tuple) for out in outs]
    return pl.pallas_call(
        body,
        out_shape=tuple(pltpu.VMEM(*out) if keep else out for out, keep in zip(outs, kept)),
        in_specs=[HBM] * len(far) + [VMEM] * len(near),
        out_specs=tuple(VMEM if keep else HBM for keep in kept),
        scratch_shapes=[pltpu.VMEM(shape, BF16) for shape in scratch]
        + [pltpu.SemaphoreType.DMA((sems,))],
        input_output_aliases=aliases or {},
        cost_estimate=pl.CostEstimate(flops=flops, bytes_accessed=moved, transcendentals=0),
        compiler_params=pltpu.CompilerParams(vmem_limit_bytes=24 * 2**20),
    )(*far, *near)


def roles():
    layer, layers = lax.axis_index("layer"), lax.axis_size("layer")
    outer = jnp.logical_or(layer == 0, layer == layers - 1)
    return outer, jnp.where(layer >= layers // 2, 1, 0)


def start(source, target, sem):
    copy = pltpu.make_async_copy(source, target, sem)
    copy.start()
    return copy


def pick(which, up_ref, down_ref, target, sem):
    @pl.when(which == 0)
    def _():
        start(up_ref, target, sem)

    @pl.when(which != 0)
    def _():
        start(down_ref, target, sem)


def arrive(target, sem):
    pltpu.make_async_copy(target, target, sem).wait()


def chunk(c, size):
    step = size // CHUNKS
    return pl.ds(pl.multiple_of(c * step, step), step)


def each_chunk(size, body):
    def one(c, carry):
        body(c, chunk(c, size))
        return carry

    lax.fori_loop(0, CHUNKS, one, 0)


def load_block(which, up_ref, down_ref, block, sems, base):
    def one(c, rows):
        pick(
            which,
            up_ref.at[0, :, rows, :],
            down_ref.at[0, :, rows, :],
            block.at[:, rows, :],
            sems.at[base + c],
        )

    each_chunk(block.shape[1], one)


def block_rows(block, rows, field, turned):
    return dot(block[0, rows, :], field[...]) + dot(block[1, rows, :], turned[...])


def dot_rows(a, b):
    return lax.dot_general(a, b, (((1,), (1,)), ((), ())), preferred_element_type=F32)


def expand(basis, coupled):
    return lax.dot_general(basis, coupled, (((0,), (0,)), ((), ())), preferred_element_type=F32)


def first_kernel(
    sup, sdn, proj, expn, coup,
    payload, pack, source1, own, expn1, couple1,
    other, after, source2, coeffs, sems,
):
    outer, first = roles()
    second = 1 - first
    k, points, total = proj.shape[2], proj.shape[3], coup.shape[4]
    owners, width = payload.shape[0], source1.shape[1]
    start(coup.at[0, first], couple1, sems.at[0])
    start(proj.at[0, first], own, sems.at[1])
    pick(first, sup.at[0], sdn.at[0], source1, sems.at[2])
    start(expn.at[0, first], expn1, sems.at[3])

    @pl.when(outer)
    def _():
        arrive(own, sems.at[1])
        arrive(source1, sems.at[2])
        coeffs[...] = dot(own[...], source1[...]).astype(BF16)
        for o in range(owners):
            start(coeffs, payload.at[o, 0, :, pl.ds(0, width)], sems.at[4])
        arrive(couple1, sems.at[0])
        arrive(expn1, sems.at[3])
        arrive(payload.at[:, 0, :, pl.ds(0, width)], sems.at[4])

    @pl.when(jnp.logical_not(outer))
    def _():
        start(proj.at[0, second], other, sems.at[5])
        start(coup.at[0, second], after, sems.at[6])
        pick(second, sup.at[0], sdn.at[0], source2, sems.at[7])
        arrive(couple1, sems.at[0])
        for o in range(owners):
            start(couple1, payload.at[o, :, :, pl.ds(0, total)], sems.at[4])
        arrive(expn1, sems.at[3])
        arrive(other, sems.at[5])
        arrive(after, sems.at[6])
        pack[:k, :points] = other[...]
        pack[2 * k :, :points] = expn1[...]
        for part in range(2):
            pack[k : 2 * k, part * total : (part + 1) * total] = after[part]
        arrive(source2, sems.at[7])
        beyond = dot(other[...], source2[...]).astype(BF16)
        pack[k : 2 * k, 2 * total : 2 * total + width] = beyond
        arrive(own, sems.at[1])
        arrive(source1, sems.at[2])
        arrive(payload.at[:, :, :, pl.ds(0, total)], sems.at[4])


def outer_apply_kernel(dup, ddn, source1, *refs):
    hops, (block, turned, result, sems) = refs[:CHUNKS], refs[CHUNKS:]
    outer, first = roles()
    load_block(first, dup, ddn, block, sems, 0)

    @pl.when(outer)
    def _():
        step = source1.shape[0] // CHUNKS
        turned[...] = rotate(source1[...])

        def one(c, rows):
            arrive(block.at[:, rows, :], sems.at[c])
            result[rows, :] = block_rows(block, rows, source1, turned).astype(BF16)

        each_chunk(source1.shape[0], one)
        for c, hop in enumerate(hops):
            hop[...] = result[c * step : (c + 1) * step, :]

    @pl.when(jnp.logical_not(outer))
    def _():
        each_chunk(
            block.shape[1], lambda c, rows: arrive(block.at[:, rows, :], sems.at[c])
        )


def inner_mix_kernel(block, packed, own, expn1, before, basis, mixed, sems):
    del sems
    outer, _ = roles()

    @pl.when(jnp.logical_not(outer))
    def _():
        k, points = own.shape
        other = packed[:k, :points]
        mixed[:, :k] = dot_rows(other, expn1[...]).astype(BF16)
        step = points // CHUNKS
        parts = [0.0, 0.0]
        for c in range(CHUNKS):
            rows = pl.ds(c * step, step)
            for part in range(2):
                columns = other[:, c * step : (c + 1) * step]
                parts[part] = parts[part] + dot(columns, block[part, rows, :])
        basis[:k, :] = own[...]
        for part in range(2):
            basis[(1 + part) * k : (2 + part) * k, :] = parts[part].astype(BF16)
        value = dot_rows(basis[...], before[...]).astype(BF16)
        for part in range(3):
            mixed[:, (1 + part) * k : (2 + part) * k] = value[part * k : (part + 1) * k, :]


def inner_prepare_kernel(*refs):
    arrived, refs = refs[:CHUNKS], refs[CHUNKS:]
    source1, basis, sums, field, turned, sems = refs
    del sems
    outer, _ = roles()

    @pl.when(jnp.logical_not(outer))
    def _():
        k, points = basis.shape[0] // 3, basis.shape[1]
        step = points // CHUNKS
        for c, part in enumerate(arrived):
            rows = slice(c * step, (c + 1) * step)
            value = (source1[rows, :].astype(F32) + part[...].astype(F32)).astype(BF16)
            field[rows, :] = value
            turned[rows, :] = rotate(value)
        sums[...] = dot(basis[: 2 * k, :], field[...])
        sums[k:, :] += dot(basis[2 * k :, :], turned[...])


def outer_couple_kernel(gathered, couple1, mixed, out, sems):
    del mixed, sems
    outer, _ = roles()

    @pl.when(outer)
    def _():
        total = couple1.shape[2]
        coeffs = gathered[:, 0, :, : out.shape[1]].reshape(total, out.shape[1])
        out[...] = (dot(couple1[0], coeffs) + dot(couple1[1], rotate(coeffs))).astype(BF16)


def inner_gather_kernel(before, sums, mixed, packed, payload, small, copies, sems):
    outer, _ = roles()

    @pl.when(jnp.logical_not(outer))
    def _():
        k, width = before.shape
        half, place = k // 2, 2 * k * payload.shape[0]
        coeffs = before[...]
        small[:k, :] = (sums[:k, :] + dot(mixed[:, k : 2 * k], coeffs)).astype(BF16)
        added = dot(mixed[:, 2 * k : 3 * k], coeffs)
        added = added + dot(mixed[:, 3 * k : 4 * k], rotate(coeffs))
        added = added + packed[k : 2 * k, place : place + width].astype(F32)
        small[k : 2 * k, :] = (sums[k:, :] + added).astype(BF16)
        small[2 * k :, :k] = mixed[:half, :k]
        small[2 * k :, k : 2 * k] = mixed[half:, :k]
        for o in range(payload.shape[0]):
            copies[o] = small[...]
        start(copies, payload, sems.at[0]).wait()


def inner_apply_kernel(sup, sdn, dup, ddn, payload, *refs):
    del payload
    arrived, refs = refs[:CHUNKS], refs[CHUNKS:]
    before, other, source1, product, trace, source2, block, turned, sems = refs
    outer, first = roles()
    pick(1 - first, sup.at[0], sdn.at[0], source2, sems.at[CHUNKS])

    @pl.when(jnp.logical_not(outer))
    def _():
        load_block(first, dup, ddn, block, sems, 0)
        points = source1.shape[0]
        step = points // CHUNKS
        added = expand(other[...], before[...])
        for c, part in enumerate(arrived):
            rows = slice(c * step, (c + 1) * step)
            value = source1[rows, :].astype(F32) + part[...].astype(F32)
            value = (value + added[rows, :]).astype(BF16)
            trace[rows, :] = value
            turned[rows, :] = rotate(value)

        def one(c, rows):
            arrive(block.at[:, rows, :], sems.at[c])
            product[rows, :] = block_rows(block, rows, trace, turned).astype(BF16)

        each_chunk(points, one)

    arrive(source2, sems.at[CHUNKS])


def inner_couple_kernel(gathered, second, packed, couple1, out, inner, later, sems):
    del sems
    outer, _ = roles()

    @pl.when(jnp.logical_not(outer))
    def _():
        owners, width = second.shape[0], second.shape[2]
        k, total = couple1.shape[1:]
        coeffs = second[:, :k, :].reshape(total, width)
        turned = rotate(coeffs)
        real = gathered[:, 0, :, :total].reshape(total, total)
        imag = gathered[:, 1, :, :total].reshape(total, total)
        inner[...] = (dot(real, coeffs) + dot(imag, turned)).astype(BF16)
        out[:k, :] = (dot(couple1[0], coeffs) + dot(couple1[1], turned)).astype(BF16)
        for o in range(owners):
            rows = slice(o * k, (o + 1) * k)
            own = inner[rows, :]
            added = [dot(second[o, 2 * k :, h * k : (h + 1) * k], own) for h in range(2)]
            added = jnp.concatenate(added, axis=0)
            later[rows, :] = (second[o, k : 2 * k, :].astype(F32) + added).astype(BF16)
        coeffs = later[...]
        result = dot(packed[k : 2 * k, :total], coeffs)
        result = result + dot(packed[k : 2 * k, total : 2 * total], rotate(coeffs))
        out[k:, :] = result.astype(BF16)


def load_part(first_chunk, which, up_ref, down_ref, block, size, sems, base):
    for c in range(block.shape[1] // size):
        source = pl.ds((first_chunk + c) * size, size)
        pick(
            which,
            up_ref.at[0, :, source, :],
            down_ref.at[0, :, source, :],
            block.at[:, pl.ds(c * size, size), :],
            sems.at[base + c],
        )


def each_chunk_of(block, size, body):
    def one(c, carry):
        body(c, pl.ds(pl.multiple_of(c * size, size), size))
        return carry

    lax.fori_loop(0, block.shape[1] // size, one, 0)


def put(which, source, up, down, sem):
    @pl.when(which == 0)
    def _():
        start(source, up.at[0], sem)

    @pl.when(which != 0)
    def _():
        start(source, down.at[0], sem)


def settle_kernel(
    expn, dup, ddn, coupled, packed, lower, bases, sems
):
    del coupled
    outer, first = roles()

    @pl.when(jnp.logical_not(outer))
    def _():
        k, points = bases.shape[0] // 2, bases.shape[1]
        start(expn.at[0, 1 - first], bases.at[pl.ds(k, k), :], sems.at[1])
        step = points // CHUNKS
        load_part(0, 1 - first, dup, ddn, lower, step, sems, 2)
        bases[:k, :] = packed[2 * k :, :points]
        arrive(bases.at[pl.ds(k, k), :], sems.at[1])
        each_chunk_of(
            lower, step, lambda c, rows: arrive(lower.at[:, rows, :], sems.at[2 + c])
        )


def inner_second_kernel(
    dup, ddn, crossed, coupled, source2, lower, bases, source1, one,
    up, down, out, trace, turned, rest, tail, added2, upper, sems,
):
    outer, first = roles()

    @pl.when(outer)
    def _():
        put(first, source1, up, down, sems.at[CHUNKS + 1])

    @pl.when(jnp.logical_not(outer))
    def _():
        put(first, one, up, down, sems.at[CHUNKS + 1])

    @pl.when(jnp.logical_not(outer))
    def _():
        k, points = coupled.shape[0] // 2, bases.shape[1]
        step = points // CHUNKS
        load_part(CHUNKS // 2, 1 - first, dup, ddn, upper, step, sems, 0)
        load_part(CHUNKS - 1, 1 - first, dup, ddn, rest, step, sems, CHUNKS)

        added = expand(bases[:k, :], coupled[:k, :])
        for c in range(CHUNKS):
            rows = slice(c * step, (c + 1) * step)
            value = source2[rows, :].astype(F32) + crossed[rows, :].astype(F32)
            value = (value + added[rows, :]).astype(BF16)
            trace[rows, :] = value
            turned[rows, :] = rotate(value)
        added2[...] = expand(bases[k:, :], coupled[k:, :]).astype(BF16)
        tail[...] = added2[points - step :, :]

        def put(block, rows, base):
            place = pl.ds(pl.multiple_of(rows.start + base, step), step)
            value = block_rows(block, rows, trace, turned) + added2[place, :].astype(F32)
            out[place, :] = value.astype(BF16)

        each_chunk_of(lower, step, lambda c, rows: put(lower, rows, 0))

        def second(c, rows):
            arrive(upper.at[:, rows, :], sems.at[c])
            put(upper, rows, points // 2)

        each_chunk_of(upper, step, second)
        arrive(rest, sems.at[CHUNKS])

    arrive(source1, sems.at[CHUNKS + 1])


def inner_rest_kernel(rest, trace, turned, tail, out, sems):
    del sems
    outer, _ = roles()

    @pl.when(jnp.logical_not(outer))
    def _():
        value = dot(rest[0], trace[...]) + dot(rest[1], turned[...])
        out[...] = (value + tail[...].astype(F32)).astype(BF16)


def last_kernel(before_up, before_down, most, last, two, source2, up, down, sums, sems):
    del before_up, before_down
    outer, first = roles()

    def put_rows(which, rows, sem):
        @pl.when(which == 0)
        def _():
            start(sums.at[rows, :], up.at[0, rows, :], sem)

        @pl.when(which != 0)
        def _():
            start(sums.at[rows, :], down.at[0, rows, :], sem)

    @pl.when(outer)
    def _():
        cut = most.shape[0]
        for part, rows in ((most, pl.ds(0, cut)), (last, pl.ds(cut, sums.shape[0] - cut))):
            value = source2[rows, :].astype(F32) + part[...].astype(F32)
            sums[rows, :] = value.astype(BF16)
            put_rows(1 - first, rows, sems.at[0])

    @pl.when(jnp.logical_not(outer))
    def _():
        put(1 - first, two, up, down, sems.at[0])

    arrive(sums, sems.at[0])


def wave(*arrays):
    layers, owners = lax.axis_size("layer"), lax.axis_size("trace")
    source_up, source_down, diag_up, diag_down, projection, expansion, coupling = (
        pltpu.with_memory_space_constraint(array, pltpu.HBM) for array in arrays
    )
    _, points, width = source_up.shape
    k, total = projection.shape[2], coupling.shape[4]
    swap = [(g, g ^ 1) for g in range(layers)]
    across = [(g, layers - 1 - g) for g in range(layers)]
    inside = across[1:-1]

    def like(*shape):
        return jax.ShapeDtypeStruct(shape, BF16)

    def kept(*shape, of=BF16):
        return shape, of

    field, block, basis, couple = (points, width), (2, points, points), (k, points), (2, k, total)
    small = dict(flops=2 * k * points * width, moved=4 * points * width)
    large = dict(flops=4 * points * points * width, moved=4 * points * points)
    diagonals = (diag_up, diag_down)
    packing = max(points, 2 * total + width)

    payload, pack, source1, own, expn1, couple1 = call(
        first_kernel,
        (
            like(owners, 2, k, max(total, width)),
            *(kept(3 * k, packing), kept(*field), kept(*basis), kept(*basis), kept(*couple)),
        ),
        (source_up, source_down, projection, expansion, coupling),
        (),
        [basis, couple, field, (k, width)],
        8,
        **small,
    )
    gathered = lax.all_to_all(payload, "trace", 0, 0)
    pairs = [(a * owners + o, b * owners + o) for a, b in inside for o in range(owners)]
    pairs += [(g * owners + o, g * owners + (o ^ 1)) for g in (0, layers - 1) for o in range(owners)]
    packed = lax.ppermute(pack, ("layer", "trace"), pairs)
    other = lax.ppermute(expn1, "layer", swap)
    *hops, block1 = call(
        outer_apply_kernel,
        (kept(points // CHUNKS, width),) * CHUNKS + (kept(*block),),
        diagonals,
        (source1,),
        [field, field],
        CHUNKS,
        **large,
    )
    arrived = [lax.ppermute(hop, "layer", swap) for hop in hops]
    basis1, mixed = call(
        inner_mix_kernel,
        (kept(3 * k, points), kept(k, 4 * k)),
        (),
        (block1, packed, own, expn1, other),
        [],
        1,
        **large,
    )
    (before,) = call(
        outer_couple_kernel, (kept(k, width),), (), (gathered, couple1, mixed), [], 1, **small
    )
    before = lax.ppermute(before, "layer", swap)
    (sums,) = call(
        inner_prepare_kernel,
        (kept(2 * k, width, of=F32),),
        (),
        (*arrived, source1, basis1),
        [field, field],
        1,
        **small,
    )
    (payload,) = call(
        inner_gather_kernel,
        (like(owners, 2 * k + k // 2, width),),
        (),
        (before, sums, mixed, packed),
        [(2 * k + k // 2, width), (owners, 2 * k + k // 2, width)],
        1,
        **small,
    )
    half = owners // 2
    ends = [[g * owners + p * half + o for g in (0, layers - 1) for o in range(half)] for p in range(2)]
    groups = [[g * owners + o for o in range(owners)] for g in range(1, layers - 1)] + ends
    second = lax.all_to_all(payload, ("layer", "trace"), 0, 0, axis_index_groups=groups)
    product, one, source2 = call(
        inner_apply_kernel,
        (kept(*field), kept(*field), kept(*field)),
        (source_up, source_down, *diagonals, payload),
        (*arrived, before, other, source1),
        [block, field],
        CHUNKS + 1,
        **large,
    )
    crossed = lax.ppermute(product, ("layer", "trace"), pairs)
    (coupled,) = call(
        inner_couple_kernel,
        (kept(2 * k, width),),
        (),
        (gathered, second, packed, couple1),
        [(total, width), (total, width)],
        1,
        **small,
    )
    reached = lax.ppermute(coupled, "layer", across)
    lower, bases = call(
        settle_kernel,
        (kept(2, points // 2, points), kept(2 * k, points)),
        (expansion, *diagonals),
        (coupled, packed),
        [],
        2 + CHUNKS // 2,
        **large,
    )
    step = points // CHUNKS
    up, down, most, two, turned, rest, tail = call(
        inner_second_kernel,
        (
            *(like(1, *field), like(1, *field)),
            *(kept(points - step, width), kept(*field), kept(*field)),
            *(kept(2, step, points), kept(step, width)),
        ),
        diagonals,
        (crossed, reached, source2, lower, bases, source1, one),
        [field, (2, points // 2 - step, points)],
        CHUNKS + 2,
        **large,
    )
    (last,) = call(
        inner_rest_kernel, (kept(step, width),), (), (rest, two, turned, tail), [], 1, **small
    )
    arrived = [lax.ppermute(part, "layer", swap) for part in (most, last)]
    return call(
        last_kernel,
        (like(1, *field), like(1, *field)),
        (up, down),
        (*arrived, two, source2),
        [field],
        1,
        aliases={0: 0, 1: 1},
        **small,
    )


def solution(mesh):
    shards = wave if mesh.shape["layer"] == ITERS + 1 else jacobi
    return jax.shard_map(
        shards,
        mesh=mesh,
        in_specs=(
            P("layer", "trace", None),
            P("layer", "trace", None),
            P("layer", None, "trace", None),
            P("layer", None, "trace", None),
            P("layer", None, None, "trace"),
            P("layer", None, None, "trace"),
            P("layer", None, None, "trace", None),
        ),
        out_specs=(P("layer", "trace", None), P("layer", "trace", None)),
        check_vma=False,
    )
```
